128 devices in a mesh: dp: 8 (over x, y_hi), seq: 16 (over z, y_lo, core).
Axes of the slice: x: 4, y: 4 (y_hi: 2, y_lo: 2; y = y_hi * 2 + y_lo), z: 4, core: 2. Of those that a mesh axis runs over, the one named last changes fastest.
Arguments:
- queries: bfloat16 [8, 4096, 2048], P('dp', 'seq'), may hold values from -32 to 32, as said below
- key_rows: bfloat16 [8, 4096, 2048], P('dp', 'seq'), may hold values from -32 to 32, as said below
- value_rows: bfloat16 [8, 4096, 2048], P('dp', 'seq'), may hold values from -6 to 6
- cotangent: bfloat16 [8, 4096, 1536], P('dp', 'seq'), may hold values from -6 to 6
- attn_gate: float32 [8, 1536], P('dp'), may hold values from -4 to 4
- lengths: int32 [8], P('dp'), may hold values from 1024 to 4096, as said below
- w_out: bfloat16 [2048, 1536], P('seq'), may hold values from -0.125 to 0.125
- row_moment: float32 [2048], P('seq'), may hold values from 1 to 30
- col_moment: float32 [1536], P('dp'), may hold values from 1 to 30
Outputs:
- grad_queries: bfloat16 [8, 4096, 2048], P('dp', 'seq')
- grad_keys: bfloat16 [8, 4096, 2048], P('dp', 'seq')
- grad_values: bfloat16 [8, 4096, 2048], P('dp', 'seq')
- grad_gate: float32 [8, 1536], P('dp')
- grad_weight: float32 [2048, 1536], P('seq', 'dp')
- row_new: float32 [2048], P('seq')
- col_new: float32 [1536], P('dp')
The draws below stay inside these ranges and needn't reach their ends.
Inputs may be any that keep to these rules, and one draw needn't show every extreme that they name: `lengths`: token slots at or beyond a sample's length are padding; some sample fills all 4096 slots. `queries`: query features. `key_rows`: key features.
All inputs are finite; a program needn't handle non-finite values.
Results may differ from the reference program's by a relative error of at most 0.019.
Values may be sent and summed in bfloat16 or wider, within the bound.
No kernel may reach another device: no remote copies, remote signals or barrier semaphores. Data moves between devices by JAX's collectives and lax.ppermute only.
A program may use at most 128 MiB of HBM per device.

```python
import math
import jax
import jax.numpy as jnp
from jax import lax

WIDTH = 1536
HEADS = 16
HEAD_DIM = 128
SEQ_LEN = 4096
BATCH = 8
INNER = 2048


def draw_queries(key, part):
    key = jax.random.fold_in(key, 11)
    return jax.random.normal(key, (BATCH, SEQ_LEN, INNER), jnp.float32).astype(jnp.bfloat16)


def draw_key_rows(key, part):
    key = jax.random.fold_in(key, 13)
    return jax.random.normal(key, (BATCH, SEQ_LEN, INNER), jnp.float32).astype(jnp.bfloat16)


def draw_lengths(key, part):
    key = jax.random.fold_in(key, 17)
    drawn = jax.random.randint(key, (BATCH,), SEQ_LEN // 4, SEQ_LEN + 1)
    chosen = jax.random.randint(jax.random.fold_in(key, 3), (), 0, BATCH)
    return jnp.where(jnp.arange(BATCH) == chosen, SEQ_LEN, drawn).astype(jnp.int32)


def level_of(key, shape, shards, smallest, largest):
    def one(dim, shards_of):
        draws = jax.random.uniform(jax.random.fold_in(jax.random.fold_in(key, 6), dim), (shards_of,), jnp.float32, smallest / len(shards), largest / len(shards))
        return jnp.repeat(jnp.exp(draws), shape[dim] // shards_of).reshape((-1,) + (1,) * (len(shape) - dim - 1))

    level = one(*shards[0])
    for cut in shards[1:]:
        level = level * one(*cut)
    return level


def noise(key, shape, spread, most, shards=(), kind=jnp.bfloat16):
    gain = level_of(key, shape, shards, -0.22, 0.18) if shards else 1.0
    values = jax.random.normal(key, shape, jnp.float32) * spread * gain
    return jnp.minimum(jnp.maximum(values, -most), most).astype(kind)


def setup_inputs(seed: int = 0) -> dict:
    streams_of = jax.random.split(jax.random.key(seed), 10)
    return {
        "queries": draw_queries(jax.random.fold_in(streams_of[9], 71), 0),
        "key_rows": draw_key_rows(jax.random.fold_in(streams_of[9], 71), 0),
        "value_rows": noise(streams_of[2], (BATCH, SEQ_LEN, INNER), 1.0, 6.0, ((0, 8), (1, 16))),
        "cotangent": noise(streams_of[3], (BATCH, SEQ_LEN, WIDTH), 1.0, 6.0, ((0, 8), (1, 16))),
        "attn_gate": noise(streams_of[4], (BATCH, WIDTH), 1.0, 4.0, ((0, 8),), jnp.float32),
        "lengths": draw_lengths(jax.random.fold_in(streams_of[9], 71), 0),
        "w_out": noise(streams_of[6], (INNER, WIDTH), INNER ** -0.5, 0.125, ((0, 16),)),
        "row_moment": jnp.clip(jnp.exp(math.log(30.0) - 3.4011974 * jax.random.uniform(streams_of[7], (INNER,), jnp.float32) ** level_of(streams_of[7], (INNER,), ((0, 16),), -0.2, 0.2)), 1.0, 30.0),
        "col_moment": jnp.clip(jnp.exp(math.log(30.0) - 3.4011974 * jax.random.uniform(streams_of[8], (WIDTH,), jnp.float32) ** level_of(streams_of[8], (WIDTH,), ((0, 8),), -0.2, 0.2)), 1.0, 30.0),
    }


epsilon = 1e-30

def head_pass(operands):
    query_rows, key_part, value_part, grad_rows, valid_len = operands
    seq_total = query_rows.shape[0]
    positions = jnp.arange(seq_total).astype(jnp.int32)
    live_slots = positions < valid_len
    score_scale = 1.0 / math.sqrt(HEAD_DIM)
    scores = jnp.dot(query_rows, key_part.T, preferred_element_type=jnp.float32) * score_scale
    scores = jnp.where(live_slots[None, :], scores, -1e+30)
    row_top = lax.optimization_barrier(jnp.max(scores, axis=1, keepdims=True))
    exponent = jnp.exp(scores - row_top)
    probs = exponent / lax.optimization_barrier(jnp.sum(exponent, axis=1, keepdims=True))
    probs = jnp.where(live_slots[:, None], probs, jnp.zeros_like(probs))
    probs_low = probs.astype(jnp.bfloat16)
    attended = jnp.dot(probs_low, value_part, preferred_element_type=jnp.float32).astype(jnp.bfloat16)
    delta = lax.optimization_barrier(jnp.sum(grad_rows.astype(jnp.float32) * attended.astype(jnp.float32), axis=1, keepdims=True))
    dprob = jnp.dot(grad_rows, value_part.T, preferred_element_type=jnp.float32)
    dscore = (probs * (dprob - delta) * score_scale).astype(jnp.bfloat16)
    grad_q = jnp.dot(dscore, key_part, preferred_element_type=jnp.float32).astype(jnp.bfloat16)
    grad_k = jnp.dot(dscore.T, query_rows, preferred_element_type=jnp.float32).astype(jnp.bfloat16)
    grad_v = jnp.dot(probs_low.T, grad_rows, preferred_element_type=jnp.float32).astype(jnp.bfloat16)
    return (grad_q, grad_k, grad_v, attended)

def reference(queries, key_rows, value_rows, cotangent, attn_gate, lengths, w_out, row_moment, col_moment):
    batch_count = queries.shape[0]
    seq_total = queries.shape[1]
    inner_dim = queries.shape[2]
    width_dim = cotangent.shape[2]
    scaled = (attn_gate[:, None, :] * cotangent.astype(jnp.float32)).astype(jnp.bfloat16)
    flat_scaled = scaled.reshape(batch_count * seq_total, width_dim)
    out_grad = jnp.dot(flat_scaled, w_out.T, preferred_element_type=jnp.float32).astype(jnp.bfloat16)

    def split_heads(source):
        shaped = source.reshape(batch_count, seq_total, HEADS, HEAD_DIM).transpose(0, 2, 1, 3)
        return shaped.reshape(batch_count * HEADS, seq_total, HEAD_DIM)

    def join_heads(source):
        shaped = source.reshape(batch_count, HEADS, seq_total, HEAD_DIM).transpose(0, 2, 1, 3)
        return shaped.reshape(batch_count, seq_total, inner_dim)
    head_lengths = jnp.repeat(lengths, HEADS).astype(jnp.int32)
    grad_q, grad_k, grad_v, attended = lax.map(head_pass, (split_heads(queries), split_heads(key_rows), split_heads(value_rows), split_heads(out_grad), head_lengths))
    flat_att = join_heads(attended).reshape(batch_count * seq_total, inner_dim)
    mixed = jnp.dot(flat_att, w_out, preferred_element_type=jnp.float32).reshape(batch_count, seq_total, width_dim)
    grad_gate = lax.optimization_barrier(jnp.sum(cotangent.astype(jnp.float32) * mixed, axis=1))
    grad_weight = jnp.dot(flat_att.T, flat_scaled, preferred_element_type=jnp.float32)
    squares = grad_weight * grad_weight + epsilon
    row_new = 0.8 * row_moment + 0.2 * lax.optimization_barrier(jnp.mean(squares, axis=1))
    col_new = 0.8 * col_moment + 0.2 * lax.optimization_barrier(jnp.mean(squares, axis=0))
    return (join_heads(grad_q), join_heads(grad_k), join_heads(grad_v), grad_gate, grad_weight, row_new, col_new)
```

```python
import jax
import jax.numpy as jnp
from jax import lax
from jax.experimental import pallas as pl
from jax.experimental.pallas import tpu as pltpu
from jax.sharding import PartitionSpec as P

HEAD_DIM = 128
SCALE = 1.0 / HEAD_DIM**0.5
LOG2E = 1.4426950408889634
EPSILON = 1e-30
BLOCK = 512
BF16 = jnp.bfloat16
F32 = jnp.float32
PARAMS = pltpu.CompilerParams(vmem_limit_bytes=56 * 2**20)


def contract(left, right, left_dim, right_dim):
    return lax.dot_general(
        left, right, (((left_dim,), (right_dim,)), ((), ())), preferred_element_type=F32
    )


def split_columns(sources):
    tokens, inner = sources[0].shape
    heads = inner // HEAD_DIM
    count = len(sources)

    def body(*refs):
        out, sems = refs[count], refs[count + 1]
        copies = []
        for which in range(count):
            for head in range(heads):
                copies.append(
                    pltpu.make_async_copy(
                        refs[which].at[:, pl.ds(head * HEAD_DIM, HEAD_DIM)],
                        out.at[head, pl.ds(which * tokens, tokens), :],
                        sems.at[which * heads + head],
                    )
                )
        for copy in copies:
            copy.start()
        for copy in copies:
            copy.wait()

    return pl.pallas_call(
        body,
        in_specs=[pl.BlockSpec(memory_space=pl.ANY)] * count,
        out_specs=pl.BlockSpec(memory_space=pl.ANY),
        out_shape=jax.ShapeDtypeStruct((heads, count * tokens, HEAD_DIM), BF16),
        scratch_shapes=[pltpu.SemaphoreType.DMA((count * heads,))],
        name="split_columns",
    )(*sources)


def join_columns(stacked, count):
    heads, rows, _ = stacked.shape
    tokens = rows // count

    def body(*refs):
        source, outs, sems = refs[0], refs[1 : 1 + count], refs[1 + count]
        copies = []
        for which in range(count):
            for head in range(heads):
                copies.append(
                    pltpu.make_async_copy(
                        source.at[head, pl.ds(which * tokens, tokens), :],
                        outs[which].at[:, pl.ds(head * HEAD_DIM, HEAD_DIM)],
                        sems.at[which * heads + head],
                    )
                )
        for copy in copies:
            copy.start()
        for copy in copies:
            copy.wait()

    return pl.pallas_call(
        body,
        in_specs=[pl.BlockSpec(memory_space=pl.ANY)],
        out_specs=[pl.BlockSpec(memory_space=pl.ANY)] * count,
        out_shape=[jax.ShapeDtypeStruct((tokens, heads * HEAD_DIM), BF16)] * count,
        scratch_shapes=[pltpu.SemaphoreType.DMA((count * heads,))],
        name="join_columns",
    )(stacked)


def forward(valid_len, packed):
    parts, rows, _ = packed.shape
    tokens = rows // 3
    total = parts * tokens
    span = BLOCK // tokens

    def body(len_ref, q_ref, k_ref, v_ref, e_ref, att_ref, qt_ref, inv_ref, kt_ref, va_ref, ka, vt):
        step = pl.program_id(0)
        length = len_ref[0]

        @pl.when(step == 0)
        def _():
            key_rows = k_ref[...].reshape(total, HEAD_DIM)
            value_rows = v_ref[...].reshape(total, HEAD_DIM)
            row = lax.broadcasted_iota(jnp.int32, (total, HEAD_DIM), 0)
            col = lax.broadcasted_iota(jnp.int32, (total, HEAD_DIM), 1)
            ka[:, :HEAD_DIM] = key_rows
            ka[:, HEAD_DIM:] = jnp.where((row >= length) & (col == 0), -1e30, 0.0).astype(BF16)
            vt[:HEAD_DIM, :] = value_rows.T
            vt[HEAD_DIM:, :] = jnp.ones((16, total), BF16)
            kt_ref[...] = key_rows.T
            va_ref[:, :HEAD_DIM] = value_rows
            va_ref[:, HEAD_DIM:] = jnp.where(col < 2, 1.0, 0.0).astype(BF16)

        query = q_ref[...].reshape(BLOCK, HEAD_DIM).T
        qt_ref[...] = query
        row = lax.broadcasted_iota(jnp.int32, (HEAD_DIM, BLOCK), 0)
        extra = jnp.where(row == 0, 1.0, 0.0).astype(BF16)
        scores = contract(ka[...], jnp.concatenate([query, extra], axis=0), 1, 0)
        top = jnp.max(scores, axis=0, keepdims=True)
        slot = step * BLOCK + lax.broadcasted_iota(jnp.int32, (1, BLOCK), 1)
        live = slot < length
        top = jnp.where(live, top * (SCALE * LOG2E), 1e30)
        low = jnp.exp2(scores * (SCALE * LOG2E) - top).astype(BF16)
        e_ref[...] = low
        summed = contract(vt[...], low, 1, 0)
        inverse = jnp.where(live, 1.0 / summed[HEAD_DIM : HEAD_DIM + 1], 0.0)
        att_ref[...] = (summed[:HEAD_DIM] * inverse).astype(BF16)
        inv_ref[...] = jnp.broadcast_to(inverse, (8, BLOCK))

    whole = lambda i, n: (0, 0)
    column = lambda i, n: (0, i)
    return pl.pallas_call(
        body,
        grid_spec=pltpu.PrefetchScalarGridSpec(
            num_scalar_prefetch=1,
            grid=(total // BLOCK,),
            in_specs=[
                pl.BlockSpec((span, tokens, HEAD_DIM), lambda i, n: (i, 0, 0)),
                pl.BlockSpec((parts, tokens, HEAD_DIM), lambda i, n: (0, 1, 0)),
                pl.BlockSpec((parts, tokens, HEAD_DIM), lambda i, n: (0, 2, 0)),
            ],
            out_specs=[
                pl.BlockSpec((total, BLOCK), column),
                pl.BlockSpec((HEAD_DIM, BLOCK), column),
                pl.BlockSpec((HEAD_DIM, BLOCK), column),
                pl.BlockSpec((8, BLOCK), column),
                pl.BlockSpec((HEAD_DIM, total), whole),
                pl.BlockSpec((total, 2 * HEAD_DIM), whole),
            ],
            scratch_shapes=[
                pltpu.VMEM((total, 2 * HEAD_DIM), BF16),
                pltpu.VMEM((HEAD_DIM + 16, total), BF16),
            ],
        ),
        out_shape=[
            jax.ShapeDtypeStruct((total, total), BF16),
            jax.ShapeDtypeStruct((HEAD_DIM, total), BF16),
            jax.ShapeDtypeStruct((HEAD_DIM, total), BF16),
            jax.ShapeDtypeStruct((8, total), F32),
            jax.ShapeDtypeStruct((HEAD_DIM, total), BF16),
            jax.ShapeDtypeStruct((total, 2 * HEAD_DIM), BF16),
        ],
        compiler_params=PARAMS,
        cost_estimate=pl.CostEstimate(
            flops=6 * total * total * HEAD_DIM,
            bytes_accessed=2 * total * total,
            transcendentals=total * total,
        ),
        name="forward",
    )(valid_len, packed, packed, packed)


def project(cotangent, gated, attended, inverse):
    total, width = cotangent.shape
    block = 1024

    def body(c_ref, w_ref, o_ref, inv_ref, g_ref, d_ref, a_ref):
        step = pl.program_id(0)
        rows = c_ref[...]
        grad = contract(w_ref[...], rows, 1, 1).astype(BF16).astype(F32)
        low = (grad * inv_ref[0:1]).astype(BF16)
        g_ref[...] = low
        out = o_ref[...]
        delta = jnp.sum(low.astype(F32) * out.astype(F32), axis=0, keepdims=True)
        d_ref[...] = jnp.broadcast_to(delta, (8, block))
        outer = contract(out, rows, 1, 0)

        @pl.when(step == 0)
        def _():
            a_ref[...] = outer

        @pl.when(step > 0)
        def _():
            a_ref[...] += outer

    column = lambda i: (0, i)
    whole = lambda i: (0, 0)
    return pl.pallas_call(
        body,
        grid=(total // block,),
        in_specs=[
            pl.BlockSpec((block, width), lambda i: (i, 0)),
            pl.BlockSpec((HEAD_DIM, width), whole),
            pl.BlockSpec((HEAD_DIM, block), column),
            pl.BlockSpec((8, block), column),
        ],
        out_specs=[
            pl.BlockSpec((HEAD_DIM, block), column),
            pl.BlockSpec((8, block), column),
            pl.BlockSpec((HEAD_DIM, width), whole),
        ],
        out_shape=[
            jax.ShapeDtypeStruct((HEAD_DIM, total), BF16),
            jax.ShapeDtypeStruct((8, total), F32),
            jax.ShapeDtypeStruct((HEAD_DIM, width), F32),
        ],
        compiler_params=PARAMS,
        cost_estimate=pl.CostEstimate(
            flops=4 * total * width * HEAD_DIM,
            bytes_accessed=2 * total * width,
            transcendentals=0,
        ),
        name="project",
    )(cotangent, gated, attended, inverse)


def backward(low, grad, delta, query, key, value, parts):
    total = low.shape[0]
    tokens = total // parts
    span = BLOCK // tokens
    last = total // BLOCK - 1

    def body(e_ref, g_ref, d_ref, q_ref, k_ref, v_ref, o_ref, dk, dv):
        step = pl.program_id(0)
        minus = -d_ref[0:1]
        high = minus.astype(BF16).astype(F32)
        row = lax.broadcasted_iota(jnp.int32, (HEAD_DIM, BLOCK), 0)
        extra = jnp.where(row == 0, high, jnp.where(row == 1, minus - high, 0.0)).astype(BF16)
        grad_block = g_ref[...]
        dprob = contract(v_ref[...], jnp.concatenate([grad_block, extra], axis=0), 1, 0)
        probs = e_ref[...]
        dscore = (probs.astype(F32) * dprob).astype(BF16)
        dq = contract(k_ref[...], dscore, 1, 0) * SCALE
        o_ref[pl.ds(step * span, span), 0:tokens, :] = (
            dq.T.astype(BF16).reshape(span, tokens, HEAD_DIM)
        )
        dv_step = contract(probs, grad_block, 1, 1)
        dk_step = contract(dscore, q_ref[...], 1, 1)

        @pl.when(step == 0)
        def _():
            dk[...] = dk_step
            dv[...] = dv_step

        @pl.when((step > 0) & (step < last))
        def _():
            dk[...] += dk_step
            dv[...] += dv_step

        @pl.when(step == last)
        def _():
            o_ref[:, tokens : 2 * tokens, :] = (
                ((dk[...] + dk_step) * SCALE).astype(BF16).reshape(parts, tokens, HEAD_DIM)
            )
            o_ref[:, 2 * tokens :, :] = (
                (dv[...] + dv_step).astype(BF16).reshape(parts, tokens, HEAD_DIM)
            )

    column = lambda i: (0, i)
    whole = lambda i: (0, 0)
    return pl.pallas_call(
        body,
        grid=(last + 1,),
        in_specs=[
            pl.BlockSpec((total, BLOCK), column),
            pl.BlockSpec((HEAD_DIM, BLOCK), column),
            pl.BlockSpec((8, BLOCK), column),
            pl.BlockSpec((HEAD_DIM, BLOCK), column),
            pl.BlockSpec((HEAD_DIM, total), whole),
            pl.BlockSpec((total, 2 * HEAD_DIM), whole),
        ],
        out_specs=pl.BlockSpec((parts, 3 * tokens, HEAD_DIM), lambda i: (0, 0, 0)),
        out_shape=jax.ShapeDtypeStruct((parts, 3 * tokens, HEAD_DIM), BF16),
        scratch_shapes=[pltpu.VMEM((total, HEAD_DIM), F32), pltpu.VMEM((total, HEAD_DIM), F32)],
        compiler_params=PARAMS,
        cost_estimate=pl.CostEstimate(
            flops=10 * total * total * HEAD_DIM,
            bytes_accessed=2 * total * total,
            transcendentals=0,
        ),
        name="backward",
    )(low, grad, delta, query, key, value)


def total_over(values, axis, size):
    spread = jnp.broadcast_to(values[None], (size,) + values.shape)
    return jnp.sum(lax.all_to_all(spread, axis, 0, 0, tiled=True), axis=0)


def shards(
    queries, key_rows, value_rows, cotangent, attn_gate, lengths, w_out, row_moment, col_moment
):
    seq_size = lax.axis_size("seq")
    dp_size = lax.axis_size("dp")
    inner_dim = queries.shape[2]
    width_dim = cotangent.shape[2]
    tokens = queries.shape[1]
    gate = attn_gate[0][None, :]
    every = lax.all_gather(cotangent[0], "seq", axis=0, tiled=True)
    packed = split_columns([queries[0], key_rows[0], value_rows[0]])
    packed = lax.all_to_all(packed, "seq", 0, 0, tiled=True)
    weight = w_out.astype(F32)
    gated = (weight * gate).astype(BF16)
    low, attended, query, inverse, key, value = forward(lengths, packed)
    grad, delta, outer = project(every, gated, attended, inverse)

    partial = (outer * gate).astype(BF16).reshape(HEAD_DIM, dp_size, width_dim // dp_size)
    partial = lax.all_to_all(partial.transpose(1, 0, 2), "dp", 0, 0, tiled=True)
    grad_weight = jnp.sum(partial.astype(F32), axis=0)
    squares = grad_weight * grad_weight + EPSILON
    gate_part = jnp.sum(weight * outer, axis=0)
    row_total = total_over(jnp.sum(squares, axis=1), "dp", dp_size)
    joined = total_over(
        jnp.concatenate([jnp.sum(squares, axis=0), gate_part]), "seq", seq_size
    )
    col_total, grad_gate = joined[: width_dim // dp_size], joined[width_dim // dp_size :]
    row_new = 0.8 * row_moment + 0.2 * (row_total / width_dim)
    col_new = 0.8 * col_moment + 0.2 * (col_total / inner_dim)

    back = backward(low, grad, delta, query, key, value, seq_size)
    back = lax.all_to_all(back, "seq", 0, 0, tiled=True)
    grad_q, grad_k, grad_v = join_columns(back, 3)
    return (
        grad_q[None],
        grad_k[None],
        grad_v[None],
        grad_gate[None],
        grad_weight,
        row_new,
        col_new,
    )


def solution(mesh):
    tokens = P("dp", "seq", None)
    return jax.shard_map(
        shards,
        mesh=mesh,
        in_specs=(
            tokens,
            tokens,
            tokens,
            tokens,
            P("dp", None),
            P("dp"),
            P("seq", None),
            P("seq"),
            P("dp"),
        ),
        out_specs=(
            tokens,
            tokens,
            tokens,
            P("dp", None),
            P("seq", "dp"),
            P("seq"),
            P("dp"),
        ),
        check_vma=False,
    )
```

```python
import jax
import jax.numpy as jnp
from jax import lax
from jax.experimental import pallas as pl
from jax.experimental.pallas import tpu as pltpu
from jax.sharding import PartitionSpec as P

HEAD_DIM = 128
SCALE = 1.0 / HEAD_DIM**0.5
LOG2E = 1.4426950408889634
EPSILON = 1e-30
BLOCK = 512
BF16 = jnp.bfloat16
F32 = jnp.float32
PARAMS = pltpu.CompilerParams(vmem_limit_bytes=56 * 2**20)


def contract(left, right, left_dim, right_dim):
    return lax.dot_general(
        left, right, (((left_dim,), (right_dim,)), ((), ())), preferred_element_type=F32
    )


def split_columns(sources):
    tokens, inner = sources[0].shape
    heads = inner // HEAD_DIM
    count = len(sources)
    block = tokens // 4

    def body(*refs):
        out = refs[count]
        for which in range(count):
            for head in range(heads):
                out[head, which] = refs[which][:, head * HEAD_DIM : (head + 1) * HEAD_DIM]

    return pl.pallas_call(
        body,
        grid=(tokens // block,),
        in_specs=[pl.BlockSpec((block, inner), lambda i: (i, 0))] * count,
        out_specs=pl.BlockSpec((heads, count, block, HEAD_DIM), lambda i: (0, 0, i, 0)),
        out_shape=jax.ShapeDtypeStruct((heads, count, tokens, HEAD_DIM), BF16),
        name="split_columns",
    )(*sources)


def join_columns(stacked):
    heads, count, tokens, _ = stacked.shape
    inner = heads * HEAD_DIM
    block = tokens // 4

    def body(*refs):
        for which in range(count):
            for head in range(heads):
                refs[1 + which][:, head * HEAD_DIM : (head + 1) * HEAD_DIM] = refs[0][head, which]

    return pl.pallas_call(
        body,
        grid=(tokens // block,),
        in_specs=[pl.BlockSpec((heads, count, block, HEAD_DIM), lambda i: (0, 0, i, 0))],
        out_specs=[pl.BlockSpec((block, inner), lambda i: (i, 0))] * count,
        out_shape=[jax.ShapeDtypeStruct((tokens, inner), BF16)] * count,
        name="join_columns",
    )(stacked)


def forward(valid_len, packed):
    parts, _, tokens, _ = packed.shape
    total = parts * tokens
    span = BLOCK // tokens

    def body(len_ref, q_ref, k_ref, v_ref, e_ref, att_ref, qt_ref, inv_ref, kt_ref, va_ref, ka, vt):
        step = pl.program_id(0)
        length = len_ref[0]

        @pl.when(step == 0)
        def _():
            key_rows = k_ref[...].reshape(total, HEAD_DIM)
            value_rows = v_ref[...].reshape(total, HEAD_DIM)
            row = lax.broadcasted_iota(jnp.int32, (total, HEAD_DIM), 0)
            col = lax.broadcasted_iota(jnp.int32, (total, HEAD_DIM), 1)
            ka[:, :HEAD_DIM] = key_rows
            ka[:, HEAD_DIM:] = jnp.where((row >= length) & (col == 0), -1e30, 0.0).astype(BF16)
            vt[:HEAD_DIM, :] = value_rows.T
            vt[HEAD_DIM:, :] = jnp.ones((16, total), BF16)
            kt_ref[...] = key_rows.T
            va_ref[:, :HEAD_DIM] = value_rows
            va_ref[:, HEAD_DIM:] = jnp.where(col < 2, 1.0, 0.0).astype(BF16)

        query = q_ref[...].reshape(BLOCK, HEAD_DIM).T
        qt_ref[...] = query
        row = lax.broadcasted_iota(jnp.int32, (HEAD_DIM, BLOCK), 0)
        extra = jnp.where(row == 0, 1.0, 0.0).astype(BF16)
        scores = contract(ka[...], jnp.concatenate([query, extra], axis=0), 1, 0)
        top = jnp.max(scores, axis=0, keepdims=True)
        slot = step * BLOCK + lax.broadcasted_iota(jnp.int32, (1, BLOCK), 1)
        live = slot < length
        top = jnp.where(live, top * (SCALE * LOG2E), 1e30)
        low = jnp.exp2(scores * (SCALE * LOG2E) - top).astype(BF16)
        e_ref[...] = low
        summed = contract(vt[...], low, 1, 0)
        inverse = jnp.where(live, 1.0 / summed[HEAD_DIM : HEAD_DIM + 1], 0.0)
        att_ref[...] = (summed[:HEAD_DIM] * inverse).astype(BF16)
        inv_ref[...] = jnp.broadcast_to(inverse, (8, BLOCK))

    whole = lambda i, n: (0, 0)
    column = lambda i, n: (0, i)
    return pl.pallas_call(
        body,
        grid_spec=pltpu.PrefetchScalarGridSpec(
            num_scalar_prefetch=1,
            grid=(total // BLOCK,),
            in_specs=[
                pl.BlockSpec((span, None, tokens, HEAD_DIM), lambda i, n: (i, 0, 0, 0)),
                pl.BlockSpec((parts, None, tokens, HEAD_DIM), lambda i, n: (0, 1, 0, 0)),
                pl.BlockSpec((parts, None, tokens, HEAD_DIM), lambda i, n: (0, 2, 0, 0)),
            ],
            out_specs=[
                pl.BlockSpec((total, BLOCK), column),
                pl.BlockSpec((HEAD_DIM, BLOCK), column),
                pl.BlockSpec((HEAD_DIM, BLOCK), column),
                pl.BlockSpec((8, BLOCK), column),
                pl.BlockSpec((HEAD_DIM, total), whole),
                pl.BlockSpec((total, 2 * HEAD_DIM), whole),
            ],
            scratch_shapes=[
                pltpu.VMEM((total, 2 * HEAD_DIM), BF16),
                pltpu.VMEM((HEAD_DIM + 16, total), BF16),
            ],
        ),
        out_shape=[
            jax.ShapeDtypeStruct((total, total), BF16),
            jax.ShapeDtypeStruct((HEAD_DIM, total), BF16),
            jax.ShapeDtypeStruct((HEAD_DIM, total), BF16),
            jax.ShapeDtypeStruct((8, total), F32),
            jax.ShapeDtypeStruct((HEAD_DIM, total), BF16),
            jax.ShapeDtypeStruct((total, 2 * HEAD_DIM), BF16),
        ],
        compiler_params=PARAMS,
        cost_estimate=pl.CostEstimate(
            flops=6 * total * total * HEAD_DIM,
            bytes_accessed=2 * total * total,
            transcendentals=total * total,
        ),
        name="forward",
    )(valid_len, packed, packed, packed)


def project(cotangent, gated, attended, inverse):
    total, width = cotangent.shape
    block = 1024

    def body(c_ref, w_ref, o_ref, inv_ref, g_ref, d_ref, a_ref):
        step = pl.program_id(0)
        rows = c_ref[...]
        grad = contract(w_ref[...], rows, 1, 1).astype(BF16).astype(F32)
        low = (grad * inv_ref[0:1]).astype(BF16)
        g_ref[...] = low
        out = o_ref[...]
        delta = jnp.sum(low.astype(F32) * out.astype(F32), axis=0, keepdims=True)
        d_ref[...] = jnp.broadcast_to(delta, (8, block))
        outer = contract(out, rows, 1, 0)

        @pl.when(step == 0)
        def _():
            a_ref[...] = outer

        @pl.when(step > 0)
        def _():
            a_ref[...] += outer

    column = lambda i: (0, i)
    whole = lambda i: (0, 0)
    return pl.pallas_call(
        body,
        grid=(total // block,),
        in_specs=[
            pl.BlockSpec((block, width), lambda i: (i, 0)),
            pl.BlockSpec((HEAD_DIM, width), whole),
            pl.BlockSpec((HEAD_DIM, block), column),
            pl.BlockSpec((8, block), column),
        ],
        out_specs=[
            pl.BlockSpec((HEAD_DIM, block), column),
            pl.BlockSpec((8, block), column),
            pl.BlockSpec((HEAD_DIM, width), whole),
        ],
        out_shape=[
            jax.ShapeDtypeStruct((HEAD_DIM, total), BF16),
            jax.ShapeDtypeStruct((8, total), F32),
            jax.ShapeDtypeStruct((HEAD_DIM, width), F32),
        ],
        compiler_params=PARAMS,
        cost_estimate=pl.CostEstimate(
            flops=4 * total * width * HEAD_DIM,
            bytes_accessed=2 * total * width,
            transcendentals=0,
        ),
        name="project",
    )(cotangent, gated, attended, inverse)


def backward(low, grad, delta, query, key, value, parts):
    total = low.shape[0]
    tokens = total // parts
    span = BLOCK // tokens
    last = total // BLOCK - 1

    def body(e_ref, g_ref, d_ref, q_ref, k_ref, v_ref, o_ref, dk, dv):
        step = pl.program_id(0)
        minus = -d_ref[0:1]
        high = minus.astype(BF16).astype(F32)
        row = lax.broadcasted_iota(jnp.int32, (HEAD_DIM, BLOCK), 0)
        extra = jnp.where(row == 0, high, jnp.where(row == 1, minus - high, 0.0)).astype(BF16)
        grad_block = g_ref[...]
        dprob = contract(v_ref[...], jnp.concatenate([grad_block, extra], axis=0), 1, 0)
        probs = e_ref[...]
        dscore = (probs.astype(F32) * dprob).astype(BF16)
        dq = contract(k_ref[...], dscore, 1, 0) * SCALE
        o_ref[pl.ds(step * span, span), 0] = (
            dq.T.astype(BF16).reshape(span, tokens, HEAD_DIM)
        )
        dv_step = contract(probs, grad_block, 1, 1)
        dk_step = contract(dscore, q_ref[...], 1, 1)

        @pl.when(step == 0)
        def _():
            dk[...] = dk_step
            dv[...] = dv_step

        @pl.when((step > 0) & (step < last))
        def _():
            dk[...] += dk_step
            dv[...] += dv_step

        @pl.when(step == last)
        def _():
            o_ref[:, 1] = (
                ((dk[...] + dk_step) * SCALE).astype(BF16).reshape(parts, tokens, HEAD_DIM)
            )
            o_ref[:, 2] = (
                (dv[...] + dv_step).astype(BF16).reshape(parts, tokens, HEAD_DIM)
            )

    column = lambda i: (0, i)
    whole = lambda i: (0, 0)
    return pl.pallas_call(
        body,
        grid=(last + 1,),
        in_specs=[
            pl.BlockSpec((total, BLOCK), column),
            pl.BlockSpec((HEAD_DIM, BLOCK), column),
            pl.BlockSpec((8, BLOCK), column),
            pl.BlockSpec((HEAD_DIM, BLOCK), column),
            pl.BlockSpec((HEAD_DIM, total), whole),
            pl.BlockSpec((total, 2 * HEAD_DIM), whole),
        ],
        out_specs=pl.BlockSpec((parts, 3, tokens, HEAD_DIM), lambda i: (0, 0, 0, 0)),
        out_shape=jax.ShapeDtypeStruct((parts, 3, tokens, HEAD_DIM), BF16),
        scratch_shapes=[pltpu.VMEM((total, HEAD_DIM), F32), pltpu.VMEM((total, HEAD_DIM), F32)],
        compiler_params=PARAMS,
        cost_estimate=pl.CostEstimate(
            flops=10 * total * total * HEAD_DIM,
            bytes_accessed=2 * total * total,
            transcendentals=0,
        ),
        name="backward",
    )(low, grad, delta, query, key, value)


def total_over(values, axis, size):
    spread = jnp.broadcast_to(values[None], (size,) + values.shape)
    return jnp.sum(lax.all_to_all(spread, axis, 0, 0, tiled=True), axis=0)


def shards(
    queries, key_rows, value_rows, cotangent, attn_gate, lengths, w_out, row_moment, col_moment
):
    seq_size = lax.axis_size("seq")
    dp_size = lax.axis_size("dp")
    inner_dim = queries.shape[2]
    width_dim = cotangent.shape[2]
    tokens = queries.shape[1]
    gate = attn_gate[0][None, :]
    every = lax.all_gather(cotangent[0], "seq", axis=0, tiled=True)
    packed = split_columns([queries[0], key_rows[0], value_rows[0]])
    packed = lax.all_to_all(packed, "seq", 0, 0, tiled=True)
    weight = w_out.astype(F32)
    gated = (weight * gate).astype(BF16)
    low, attended, query, inverse, key, value = forward(lengths, packed)
    grad, delta, outer = project(every, gated, attended, inverse)

    partial = (outer * gate).astype(BF16).reshape(HEAD_DIM, dp_size, width_dim // dp_size)
    partial = lax.all_to_all(partial.transpose(1, 0, 2), "dp", 0, 0, tiled=True)
    back = backward(low, grad, delta, query, key, value, seq_size)
    back, partial = lax.optimization_barrier((back, partial))
    grad_weight = jnp.sum(partial.astype(F32), axis=0)
    squares = grad_weight * grad_weight + EPSILON
    gate_part = jnp.sum(weight * outer, axis=0)
    row_total = total_over(jnp.sum(squares, axis=1), "dp", dp_size)
    joined = total_over(
        jnp.concatenate([jnp.sum(squares, axis=0), gate_part]), "seq", seq_size
    )
    col_total, grad_gate = joined[: width_dim // dp_size], joined[width_dim // dp_size :]
    row_new = 0.8 * row_moment + 0.2 * (row_total / width_dim)
    col_new = 0.8 * col_moment + 0.2 * (col_total / inner_dim)
    back = lax.all_to_all(back, "seq", 0, 0, tiled=True)
    grad_q, grad_k, grad_v = join_columns(back)
    return (
        grad_q[None],
        grad_k[None],
        grad_v[None],
        grad_gate[None],
        grad_weight,
        row_new,
        col_new,
    )


def solution(mesh):
    tokens = P("dp", "seq", None)
    return jax.shard_map(
        shards,
        mesh=mesh,
        in_specs=(
            tokens,
            tokens,
            tokens,
            tokens,
            P("dp", None),
            P("dp"),
            P("seq", None),
            P("seq"),
            P("dp"),
        ),
        out_specs=(
            tokens,
            tokens,
            tokens,
            P("dp", None),
            P("seq", "dp"),
            P("seq"),
            P("dp"),
        ),
        check_vma=False,
    )
```

```python
import jax
import jax.numpy as jnp
from jax import lax
from jax.experimental import pallas as pl
from jax.experimental.pallas import tpu as pltpu
from jax.sharding import PartitionSpec as P

HEAD_DIM = 128
SCALE = 1.0 / HEAD_DIM**0.5
LOG2E = 1.4426950408889634
EPSILON = 1e-30
BLOCK = 512
HALVES = 2
BF16 = jnp.bfloat16
F32 = jnp.float32
PARAMS = pltpu.CompilerParams(vmem_limit_bytes=56 * 2**20)


def contract(left, right, left_dim, right_dim):
    return lax.dot_general(
        left, right, (((left_dim,), (right_dim,)), ((), ())), preferred_element_type=F32
    )


def split_columns(sources):
    tokens, inner = sources[0].shape
    heads = inner // HEAD_DIM
    count = len(sources)
    block = tokens // 4

    def body(*refs):
        out = refs[count]
        for which in range(count):
            for head in range(heads):
                out[head, which] = refs[which][:, head * HEAD_DIM : (head + 1) * HEAD_DIM]

    return pl.pallas_call(
        body,
        grid=(tokens // block,),
        in_specs=[pl.BlockSpec((block, inner), lambda i: (i, 0))] * count,
        out_specs=pl.BlockSpec((heads, count, block, HEAD_DIM), lambda i: (0, 0, i, 0)),
        out_shape=jax.ShapeDtypeStruct((heads, count, tokens, HEAD_DIM), BF16),
        name="split_columns",
    )(*sources)


def join_columns(stacked):
    heads, count, tokens, _ = stacked.shape
    inner = heads * HEAD_DIM
    block = tokens // 4

    def body(*refs):
        rows = pl.ds(pl.program_id(0) * block, block)
        for which in range(count):
            for head in range(heads):
                refs[1 + which][:, head * HEAD_DIM : (head + 1) * HEAD_DIM] = refs[0][
                    head, which, rows, :
                ]

    return pl.pallas_call(
        body,
        grid=(tokens // block,),
        in_specs=[pl.BlockSpec(memory_space=pltpu.VMEM)],
        out_specs=[pl.BlockSpec((block, inner), lambda i: (i, 0))] * count,
        out_shape=[jax.ShapeDtypeStruct((tokens, inner), BF16)] * count,
        name="join_columns",
    )(stacked)


def forward(valid_len, packed):
    parts, _, tokens, _ = packed.shape
    total = parts * tokens
    half = tokens // HALVES
    span = BLOCK // half
    steps = total // BLOCK
    chunk = 512

    def body(
        len_ref, p_ref, e_ref, att_ref, qt_ref, inv_ref, kt_ref, va_ref, ka, vt, held, tops
    ):
        step = pl.program_id(0)
        length = len_ref[0]

        @pl.when(step == 0)
        def _():
            key_rows = p_ref[:, 1].reshape(total, HEAD_DIM)
            value_rows = p_ref[:, 2].reshape(total, HEAD_DIM)
            row = lax.broadcasted_iota(jnp.int32, (total, HEAD_DIM), 0)
            col = lax.broadcasted_iota(jnp.int32, (total, HEAD_DIM), 1)
            ka[:, :HEAD_DIM] = key_rows
            ka[:, HEAD_DIM:] = jnp.where((row >= length) & (col == 0), -1e30, 0.0).astype(BF16)
            vt[:HEAD_DIM, :] = value_rows.T
            vt[HEAD_DIM:, :] = jnp.ones((16, total), BF16)
            kt_ref[...] = key_rows.T
            va_ref[:, :HEAD_DIM] = value_rows
            va_ref[:, HEAD_DIM:] = jnp.where(col < 2, 1.0, 0.0).astype(BF16)

        def live(block):
            lane = lax.broadcasted_iota(jnp.int32, (1, BLOCK), 1)
            per_half = parts // span
            part = (block % per_half) * span + lane // half
            return part * tokens + (block // per_half) * half + lane % half < length

        def work(score_next, weigh_last):
            if score_next:
                per_half = parts // span
                query = p_ref[
                    pl.ds(step % per_half * span, span), 0, pl.ds(step // per_half * half, half), :
                ]
                query = query.reshape(BLOCK, HEAD_DIM).T
                qt_ref[...] = query
                row = lax.broadcasted_iota(jnp.int32, (HEAD_DIM, BLOCK), 0)
                extra = jnp.where(row == 0, 1.0, 0.0).astype(BF16)
                widened = jnp.concatenate([query, extra], axis=0)
                top = jnp.full((8, BLOCK), -3e38, F32)
            if weigh_last:
                shift = tops[0:1]
                summed = jnp.zeros((HEAD_DIM + 16, BLOCK), F32)
            for first in range(0, total, chunk):
                rows = slice(first, first + chunk)
                if weigh_last:
                    low = jnp.exp2(held[rows, :] * (SCALE * LOG2E) - shift).astype(BF16)
                    e_ref[rows, :] = low
                if score_next:
                    scores = contract(ka[rows, :], widened, 1, 0)
                    held[rows, :] = scores
                    top = jnp.maximum(top, jnp.max(scores.reshape(chunk // 8, 8, BLOCK), axis=0))
                if weigh_last:
                    summed = summed + contract(vt[:, rows], low, 1, 0)
            if weigh_last:
                inverse = jnp.where(live(step - 1), 1.0 / summed[HEAD_DIM : HEAD_DIM + 1], 0.0)
                att_ref[...] = (summed[:HEAD_DIM] * inverse).astype(BF16)
                inv_ref[...] = jnp.broadcast_to(inverse, (8, BLOCK))
            if score_next:
                top = jnp.max(top, axis=0, keepdims=True) * (SCALE * LOG2E)
                tops[...] = jnp.broadcast_to(jnp.where(live(step), top, 1e30), (8, BLOCK))

        pl.when(step == 0)(lambda: work(True, False))
        pl.when((step > 0) & (step < steps))(lambda: work(True, True))
        pl.when(step == steps)(lambda: work(False, True))

    whole = lambda i, n: (0, 0)
    scored = lambda i, n: (0, jnp.minimum(i, steps - 1))
    weighed = lambda i, n: (0, jnp.maximum(i - 1, 0))
    return pl.pallas_call(
        body,
        grid_spec=pltpu.PrefetchScalarGridSpec(
            num_scalar_prefetch=1,
            grid=(steps + 1,),
            in_specs=[
                pl.BlockSpec(memory_space=pltpu.VMEM),
            ],
            out_specs=[
                pl.BlockSpec((total, BLOCK), weighed),
                pl.BlockSpec((HEAD_DIM, BLOCK), weighed),
                pl.BlockSpec((HEAD_DIM, BLOCK), scored),
                pl.BlockSpec((8, BLOCK), weighed),
                pl.BlockSpec((HEAD_DIM, total), whole),
                pl.BlockSpec((total, 2 * HEAD_DIM), whole),
            ],
            scratch_shapes=[
                pltpu.VMEM((total, 2 * HEAD_DIM), BF16),
                pltpu.VMEM((HEAD_DIM + 16, total), BF16),
                pltpu.VMEM((total, BLOCK), F32),
                pltpu.VMEM((8, BLOCK), F32),
            ],
        ),
        out_shape=[
            jax.ShapeDtypeStruct((total, total), BF16),
            jax.ShapeDtypeStruct((HEAD_DIM, total), BF16),
            jax.ShapeDtypeStruct((HEAD_DIM, total), BF16),
            jax.ShapeDtypeStruct((8, total), F32),
            jax.ShapeDtypeStruct((HEAD_DIM, total), BF16),
            jax.ShapeDtypeStruct((total, 2 * HEAD_DIM), BF16),
        ],
        compiler_params=PARAMS,
        cost_estimate=pl.CostEstimate(
            flops=6 * total * total * HEAD_DIM,
            bytes_accessed=2 * total * total,
            transcendentals=total * total,
        ),
        name="forward",
    )(valid_len, packed)


def project(which, cotangent, gated, attended, inverse):
    count, width = cotangent.shape
    block = 1024
    steps = count // block

    def body(c_ref, w_ref, o_ref, inv_ref, g_ref, d_ref, a_ref):
        step = pl.program_id(0)
        rows = c_ref[...]
        grad = contract(w_ref[...], rows, 1, 1).astype(BF16).astype(F32)
        low = (grad * inv_ref[0:1]).astype(BF16)
        g_ref[...] = low
        out = o_ref[...]
        delta = jnp.sum(low.astype(F32) * out.astype(F32), axis=0, keepdims=True)
        d_ref[...] = jnp.broadcast_to(delta, (8, block))
        outer = contract(out, rows, 1, 0)

        @pl.when(step == 0)
        def _():
            a_ref[...] = outer

        @pl.when(step > 0)
        def _():
            a_ref[...] += outer

    column = lambda i: (0, i)
    shifted = lambda i: (0, i + which * steps)
    whole = lambda i: (0, 0)
    return pl.pallas_call(
        body,
        grid=(steps,),
        in_specs=[
            pl.BlockSpec((block, width), lambda i: (i, 0)),
            pl.BlockSpec((HEAD_DIM, width), whole),
            pl.BlockSpec((HEAD_DIM, block), shifted),
            pl.BlockSpec((8, block), shifted),
        ],
        out_specs=[
            pl.BlockSpec((HEAD_DIM, block), column),
            pl.BlockSpec((8, block), column),
            pl.BlockSpec((HEAD_DIM, width), whole),
        ],
        out_shape=[
            jax.ShapeDtypeStruct((HEAD_DIM, count), BF16),
            jax.ShapeDtypeStruct((8, count), F32),
            jax.ShapeDtypeStruct((HEAD_DIM, width), F32),
        ],
        compiler_params=PARAMS,
        cost_estimate=pl.CostEstimate(
            flops=4 * count * width * HEAD_DIM,
            bytes_accessed=2 * count * width,
            transcendentals=0,
        ),
        name="project",
    )(cotangent, gated, attended, inverse)


def backward(which, low, grad, delta, query, key, value, parts, earlier):
    total = low.shape[0]
    tokens = total // parts
    half = tokens // HALVES
    span = BLOCK // half
    steps = grad.shape[1] // BLOCK
    chunk = 1024
    final = which == HALVES - 1
    n_in = 6 + len(earlier)

    def body(*refs):
        e_ref, g_ref, d_ref, q_ref, k_ref, v_ref = refs[:6]
        before = refs[6:n_in]
        if final:
            o_ref, dk, dv = refs[n_in:]
        else:
            dq_ref, dk, dv = refs[n_in:]
        step = pl.program_id(0)

        @pl.when(step == 0)
        def _():
            if before:
                dk[...] = before[-2][...]
                dv[...] = before[-1][...]
            else:
                dk[...] = jnp.zeros_like(dk)
                dv[...] = jnp.zeros_like(dv)

        minus = -d_ref[0:1]
        high = minus.astype(BF16).astype(F32)
        row = lax.broadcasted_iota(jnp.int32, (HEAD_DIM, BLOCK), 0)
        extra = jnp.where(row == 0, high, jnp.where(row == 1, minus - high, 0.0)).astype(BF16)
        grad_block = g_ref[...]
        widened = jnp.concatenate([grad_block, extra], axis=0)
        grad_rows = grad_block.T
        query_rows = q_ref[...].T
        dq = jnp.zeros((HEAD_DIM, BLOCK), F32)
        for first in range(0, total, chunk):
            rows = slice(first, first + chunk)
            dprob = contract(v_ref[rows, :], widened, 1, 0)
            probs = e_ref[rows, :]
            dscore = (probs.astype(F32) * dprob).astype(BF16)
            dq = dq + contract(k_ref[:, rows], dscore, 1, 0)
            dv[rows, :] += contract(probs, grad_rows, 1, 0)
            dk[rows, :] += contract(dscore, query_rows, 1, 0)
        dq = (dq * SCALE).T.astype(BF16).reshape(span, half, HEAD_DIM)
        at = pl.ds(step * span, span)
        if final:
            o_ref[at, 0, which * half : (which + 1) * half, :] = dq

            @pl.when(step == steps - 1)
            def _():
                for index in range(which):
                    o_ref[:, 0, index * half : (index + 1) * half, :] = before[index][...]
                o_ref[:, 1] = (dk[...] * SCALE).astype(BF16).reshape(parts, tokens, HEAD_DIM)
                o_ref[:, 2] = dv[...].astype(BF16).reshape(parts, tokens, HEAD_DIM)

        else:
            dq_ref[at] = dq

    column = lambda i: (0, i)
    shifted = lambda i: (0, i + which * steps)
    whole = lambda i: (0, 0)
    sums = jax.ShapeDtypeStruct((total, HEAD_DIM), F32)
    if final:
        out_specs = pl.BlockSpec((parts, 3, tokens, HEAD_DIM), lambda i: (0, 0, 0, 0))
        out_shape = jax.ShapeDtypeStruct((parts, 3, tokens, HEAD_DIM), BF16)
        scratch = [pltpu.VMEM((total, HEAD_DIM), F32)] * 2
    else:
        out_specs = [
            pl.BlockSpec((parts, half, HEAD_DIM), lambda i: (0, 0, 0)),
            pl.BlockSpec((total, HEAD_DIM), whole),
            pl.BlockSpec((total, HEAD_DIM), whole),
        ]
        out_shape = [jax.ShapeDtypeStruct((parts, half, HEAD_DIM), BF16), sums, sums]
        scratch = []
    return pl.pallas_call(
        body,
        grid=(steps,),
        in_specs=[
            pl.BlockSpec((total, BLOCK), shifted),
            pl.BlockSpec((HEAD_DIM, BLOCK), column),
            pl.BlockSpec((8, BLOCK), column),
            pl.BlockSpec((HEAD_DIM, BLOCK), shifted),
            pl.BlockSpec((HEAD_DIM, total), whole),
            pl.BlockSpec((total, 2 * HEAD_DIM), whole),
        ]
        + [
            pl.BlockSpec(memory_space=pltpu.VMEM) for _ in earlier
        ],
        out_specs=out_specs,
        out_shape=out_shape,
        scratch_shapes=scratch,
        compiler_params=PARAMS,
        cost_estimate=pl.CostEstimate(
            flops=10 * total * total * HEAD_DIM // HALVES,
            bytes_accessed=2 * total * total // HALVES,
            transcendentals=0,
        ),
        name="backward",
    )(low, grad, delta, query, key, value, *earlier)


def swap(values, axis, size, bit):
    return lax.ppermute(values, axis, [(i, i ^ bit) for i in range(size)])


def total_over(values, axis, size):
    bit = 1
    while bit < size:
        values = values + swap(values, axis, size, bit)
        bit *= 2
    return values


def scatter_over(values, axis, size):
    bit = size // 2
    while bit:
        upper = lax.axis_index(axis) // bit % 2
        keep = lax.dynamic_slice_in_dim(values, upper * bit, bit, 0)
        give = lax.dynamic_slice_in_dim(values, (1 - upper) * bit, bit, 0)
        values = keep + swap(give, axis, size, bit)
        bit //= 2
    return values[0]


def shards(
    queries, key_rows, value_rows, cotangent, attn_gate, lengths, w_out, row_moment, col_moment
):
    seq_size = lax.axis_size("seq")
    dp_size = lax.axis_size("dp")
    inner_dim = queries.shape[2]
    width_dim = cotangent.shape[2]
    columns = width_dim // dp_size
    half = queries.shape[1] // HALVES
    gate = attn_gate[0][None, :]
    every = [
        lax.all_gather(cotangent[0, i * half : (i + 1) * half], "seq", axis=0, tiled=True)
        for i in range(HALVES)
    ]
    packed = split_columns([queries[0], key_rows[0], value_rows[0]])
    packed = lax.all_to_all(packed, "seq", 0, 0, tiled=True)
    weight = w_out.astype(F32)
    gated = (weight * gate).astype(BF16)
    low, attended, query, inverse, key, value = forward(lengths, packed)

    earlier, sums, outer = [], [], 0.0
    for which in range(HALVES):
        grad, delta, part = project(which, every[which], gated, attended, inverse)
        outer = outer + part
        back = backward(
            which, low, grad, delta, query, key, value, seq_size, earlier + sums
        )
        if which < HALVES - 1:
            earlier.append(back[0])
            sums = list(back[1:])
    back = lax.all_to_all(back, "seq", 0, 0, tiled=True)

    partial = (outer * gate).reshape(HEAD_DIM, dp_size, columns).transpose(1, 0, 2)
    grad_weight = scatter_over(partial, "dp", dp_size)
    squares = grad_weight * grad_weight + EPSILON
    gate_part = jnp.sum(weight * outer, axis=0)
    row_total = total_over(jnp.sum(squares, axis=1), "dp", dp_size)
    joined = jnp.concatenate([jnp.sum(squares, axis=0), gate_part])
    joined = total_over(joined, "seq", seq_size)
    row_new = 0.8 * row_moment + 0.2 * (row_total / width_dim)
    col_new = 0.8 * col_moment + 0.2 * (joined[:columns] / inner_dim)
    grad_q, grad_k, grad_v = join_columns(back)
    return (
        grad_q[None],
        grad_k[None],
        grad_v[None],
        joined[columns:][None],
        grad_weight,
        row_new,
        col_new,
    )


def solution(mesh):
    tokens = P("dp", "seq", None)
    return jax.shard_map(
        shards,
        mesh=mesh,
        in_specs=(
            tokens,
            tokens,
            tokens,
            tokens,
            P("dp", None),
            P("dp"),
            P("seq", None),
            P("seq"),
            P("dp"),
        ),
        out_specs=(
            tokens,
            tokens,
            tokens,
            P("dp", None),
            P("seq", "dp"),
            P("seq"),
            P("dp"),
        ),
        check_vma=False,
    )
```

```python
import jax
import jax.numpy as jnp
from jax import lax
from jax.experimental import pallas as pl
from jax.experimental.pallas import tpu as pltpu
from jax.sharding import PartitionSpec as P

HEAD_DIM = 128
SCALE = 1.0 / HEAD_DIM**0.5
LOG2E = 1.4426950408889634
EPSILON = 1e-30
BLOCK = 512
BF16 = jnp.bfloat16
F32 = jnp.float32
PARAMS = pltpu.CompilerParams(vmem_limit_bytes=40 * 2**20)


def contract(left, right, left_dim, right_dim):
    return lax.dot_general(
        left, right, (((left_dim,), (right_dim,)), ((), ())), preferred_element_type=F32
    )


def split_columns(sources):
    tokens, inner = sources[0].shape
    heads = inner // HEAD_DIM
    count = len(sources)
    block = tokens // 4

    def body(*refs):
        out = refs[count]
        for which in range(count):
            for head in range(heads):
                out[head, which] = refs[which][:, head * HEAD_DIM : (head + 1) * HEAD_DIM]

    return pl.pallas_call(
        body,
        grid=(tokens // block,),
        in_specs=[pl.BlockSpec((block, inner), lambda i: (i, 0))] * count,
        out_specs=pl.BlockSpec((heads, count, block, HEAD_DIM), lambda i: (0, 0, i, 0)),
        out_shape=jax.ShapeDtypeStruct((heads, count, tokens, HEAD_DIM), BF16),
        name="split_columns",
    )(*sources)


def join_columns(stacked):
    heads, count, tokens, _ = stacked.shape
    inner = heads * HEAD_DIM
    block = tokens // 4

    def body(*refs):
        rows = pl.ds(pl.program_id(0) * block, block)
        for which in range(count):
            for head in range(heads):
                refs[1 + which][:, head * HEAD_DIM : (head + 1) * HEAD_DIM] = refs[0][
                    head, which, rows, :
                ]

    return pl.pallas_call(
        body,
        grid=(tokens // block,),
        in_specs=[pl.BlockSpec(memory_space=pltpu.VMEM)],
        out_specs=[pl.BlockSpec((block, inner), lambda i: (i, 0))] * count,
        out_shape=[jax.ShapeDtypeStruct((tokens, inner), BF16)] * count,
        compiler_params=pltpu.CompilerParams(vmem_limit_bytes=12 * 2**20),
        name="join_columns",
    )(stacked)


def forward(valid_len, packed):
    parts, _, tokens, _ = packed.shape
    total = parts * tokens
    span = BLOCK // tokens
    steps = total // BLOCK
    chunk = 512

    def body(
        len_ref, p_ref, e_ref, att_ref, qt_ref, inv_ref, kt_ref, va_ref, ka, vt, held, tops
    ):
        step = pl.program_id(0)
        length = len_ref[0]

        @pl.when(step == 0)
        def _():
            key_rows = p_ref[:, 1].reshape(total, HEAD_DIM)
            value_rows = p_ref[:, 2].reshape(total, HEAD_DIM)
            row = lax.broadcasted_iota(jnp.int32, (total, HEAD_DIM), 0)
            col = lax.broadcasted_iota(jnp.int32, (total, HEAD_DIM), 1)
            ka[:, :HEAD_DIM] = key_rows
            ka[:, HEAD_DIM:] = jnp.where((row >= length) & (col == 0), -1e30, 0.0).astype(BF16)
            vt[:HEAD_DIM, :] = value_rows.T
            vt[HEAD_DIM:, :] = jnp.ones((16, total), BF16)
            kt_ref[...] = key_rows.T
            va_ref[:, :HEAD_DIM] = value_rows
            va_ref[:, HEAD_DIM:] = jnp.where(col < 2, 1.0, 0.0).astype(BF16)

        def live(block):
            slot = block * BLOCK + lax.broadcasted_iota(jnp.int32, (1, BLOCK), 1)
            return slot < length

        def work(score_next, weigh_last):
            if score_next:
                query = p_ref[pl.ds(step * span, span), 0]
                query = query.reshape(BLOCK, HEAD_DIM).T
                qt_ref[...] = query
                row = lax.broadcasted_iota(jnp.int32, (HEAD_DIM, BLOCK), 0)
                extra = jnp.where(row == 0, 1.0, 0.0).astype(BF16)
                widened = jnp.concatenate([query, extra], axis=0)
                top = jnp.full((8, BLOCK), -3e38, F32)
            if weigh_last:
                shift = tops[0:1]
                summed = jnp.zeros((HEAD_DIM + 16, BLOCK), F32)
            for first in range(0, total, chunk):
                rows = slice(first, first + chunk)
                if weigh_last:
                    low = jnp.exp2(held[rows, :] * (SCALE * LOG2E) - shift).astype(BF16)
                    e_ref[rows, :] = low
                if score_next:
                    scores = contract(ka[rows, :], widened, 1, 0)
                    held[rows, :] = scores
                    top = jnp.maximum(top, jnp.max(scores.reshape(chunk // 8, 8, BLOCK), axis=0))
                if weigh_last:
                    summed = summed + contract(vt[:, rows], low, 1, 0)
            if weigh_last:
                inverse = jnp.where(live(step - 1), 1.0 / summed[HEAD_DIM : HEAD_DIM + 1], 0.0)
                att_ref[...] = (summed[:HEAD_DIM] * inverse).astype(BF16)
                inv_ref[...] = jnp.broadcast_to(inverse, (8, BLOCK))
            if score_next:
                top = jnp.max(top, axis=0, keepdims=True) * (SCALE * LOG2E)
                tops[...] = jnp.broadcast_to(jnp.where(live(step), top, 1e30), (8, BLOCK))

        pl.when(step == 0)(lambda: work(True, False))
        pl.when((step > 0) & (step < steps))(lambda: work(True, True))
        pl.when(step == steps)(lambda: work(False, True))

    whole = lambda i, n: (0, 0)
    scored = lambda i, n: (0, jnp.minimum(i, steps - 1))
    weighed = lambda i, n: (0, jnp.maximum(i - 1, 0))
    return pl.pallas_call(
        body,
        grid_spec=pltpu.PrefetchScalarGridSpec(
            num_scalar_prefetch=1,
            grid=(steps + 1,),
            in_specs=[
                pl.BlockSpec(memory_space=pltpu.VMEM),
            ],
            out_specs=[
                pl.BlockSpec((total, BLOCK), weighed),
                pl.BlockSpec((HEAD_DIM, BLOCK), weighed),
                pl.BlockSpec((HEAD_DIM, BLOCK), scored),
                pl.BlockSpec((8, BLOCK), weighed),
                pl.BlockSpec((HEAD_DIM, total), whole),
                pl.BlockSpec((total, 2 * HEAD_DIM), whole),
            ],
            scratch_shapes=[
                pltpu.VMEM((total, 2 * HEAD_DIM), BF16),
                pltpu.VMEM((HEAD_DIM + 16, total), BF16),
                pltpu.VMEM((total, BLOCK), F32),
                pltpu.VMEM((8, BLOCK), F32),
            ],
        ),
        out_shape=[
            jax.ShapeDtypeStruct((total, total), BF16),
            jax.ShapeDtypeStruct((HEAD_DIM, total), BF16),
            jax.ShapeDtypeStruct((HEAD_DIM, total), BF16),
            jax.ShapeDtypeStruct((8, total), F32),
            jax.ShapeDtypeStruct((HEAD_DIM, total), BF16),
            jax.ShapeDtypeStruct((total, 2 * HEAD_DIM), BF16),
        ],
        compiler_params=PARAMS,
        cost_estimate=pl.CostEstimate(
            flops=6 * total * total * HEAD_DIM,
            bytes_accessed=2 * total * total,
            transcendentals=total * total,
        ),
        name="forward",
    )(valid_len, packed)


def project(places, pieces, gated, attended, inverse):
    width = gated.shape[1]
    total = attended.shape[1]
    count = len(pieces)

    def body(*refs):
        place_ref, sources = refs[0], refs[1 : 1 + count]
        w_ref, o_ref, inv_ref, g_ref, d_ref, a_ref = refs[1 + count : 7 + count]
        buffers, sems = refs[7 + count : 7 + 2 * count], refs[7 + 2 * count]
        copies = [
            pltpu.make_async_copy(sources[i], buffers[i], sems.at[i]) for i in range(count)
        ]
        for copy in copies:
            copy.start()
        outer = jnp.zeros((HEAD_DIM, width), F32)
        for i in range(count):
            size = pieces[i][0].shape[0]
            lanes = pl.ds(pl.multiple_of(place_ref[pieces[i][1]], HEAD_DIM), size)
            copies[i].wait()
            rows = buffers[i][...]
            grad = contract(w_ref[...], rows, 1, 1).astype(BF16).astype(F32)
            low = (grad * inv_ref[0:1, lanes]).astype(BF16)
            g_ref[:, lanes] = low
            out = o_ref[:, lanes]
            delta = jnp.sum(low.astype(F32) * out.astype(F32), axis=0, keepdims=True)
            d_ref[:, lanes] = jnp.broadcast_to(delta, (8, size))
            outer = outer + contract(out, rows, 1, 0)
        a_ref[...] = outer

    vmem = pl.BlockSpec(memory_space=pltpu.VMEM)
    return pl.pallas_call(
        body,
        in_specs=[pl.BlockSpec(memory_space=pltpu.SMEM)]
        + [pl.BlockSpec(memory_space=pl.ANY)] * count
        + [vmem] * 3,
        out_specs=[vmem] * 3,
        out_shape=[
            jax.ShapeDtypeStruct((HEAD_DIM, total), BF16),
            jax.ShapeDtypeStruct((8, total), F32),
            jax.ShapeDtypeStruct((HEAD_DIM, width), F32),
        ],
        scratch_shapes=[pltpu.VMEM(rows.shape, BF16) for rows, _ in pieces]
        + [pltpu.SemaphoreType.DMA((count,))],
        compiler_params=PARAMS,
        cost_estimate=pl.CostEstimate(
            flops=4 * total * width * HEAD_DIM,
            bytes_accessed=2 * total * width,
            transcendentals=0,
        ),
        name="project",
    )(places, *[rows for rows, _ in pieces], gated, attended, inverse)


def backward(low, grad, delta, query, key, value, parts):
    total = low.shape[0]
    tokens = total // parts
    span = BLOCK // tokens
    steps = total // BLOCK
    chunk = 1024

    def body(e_ref, g_ref, d_ref, q_ref, k_ref, v_ref, o_ref, dk, dv):
        step = pl.program_id(0)

        @pl.when(step == 0)
        def _():
            dk[...] = jnp.zeros_like(dk)
            dv[...] = jnp.zeros_like(dv)

        minus = -d_ref[0:1]
        high = minus.astype(BF16).astype(F32)
        row = lax.broadcasted_iota(jnp.int32, (HEAD_DIM, BLOCK), 0)
        extra = jnp.where(row == 0, high, jnp.where(row == 1, minus - high, 0.0)).astype(BF16)
        grad_block = g_ref[...]
        widened = jnp.concatenate([grad_block, extra], axis=0)
        grad_rows = grad_block.T
        query_rows = q_ref[...].T
        dq = jnp.zeros((HEAD_DIM, BLOCK), F32)
        for first in range(0, total, chunk):
            rows = slice(first, first + chunk)
            dprob = contract(v_ref[rows, :], widened, 1, 0)
            probs = e_ref[rows, :]
            dscore = (probs.astype(F32) * dprob).astype(BF16)
            dq = dq + contract(k_ref[:, rows], dscore, 1, 0)
            dv[rows, :] += contract(probs, grad_rows, 1, 0)
            dk[rows, :] += contract(dscore, query_rows, 1, 0)
        dq = (dq * SCALE).T.astype(BF16).reshape(span, tokens, HEAD_DIM)
        o_ref[pl.ds(step * span, span), 0] = dq

        @pl.when(step == steps - 1)
        def _():
            o_ref[:, 1] = (dk[...] * SCALE).astype(BF16).reshape(parts, tokens, HEAD_DIM)
            o_ref[:, 2] = dv[...].astype(BF16).reshape(parts, tokens, HEAD_DIM)

    column = lambda i: (0, i)
    whole = lambda i: (0, 0)
    return pl.pallas_call(
        body,
        grid=(steps,),
        in_specs=[
            pl.BlockSpec((total, BLOCK), column),
            pl.BlockSpec((HEAD_DIM, BLOCK), column),
            pl.BlockSpec((8, BLOCK), column),
            pl.BlockSpec((HEAD_DIM, BLOCK), column),
            pl.BlockSpec((HEAD_DIM, total), whole),
            pl.BlockSpec((total, 2 * HEAD_DIM), whole),
        ],
        out_specs=pl.BlockSpec((parts, 3, tokens, HEAD_DIM), lambda i: (0, 0, 0, 0)),
        out_shape=jax.ShapeDtypeStruct((parts, 3, tokens, HEAD_DIM), BF16),
        scratch_shapes=[pltpu.VMEM((total, HEAD_DIM), F32)] * 2,
        compiler_params=PARAMS,
        cost_estimate=pl.CostEstimate(
            flops=10 * total * total * HEAD_DIM,
            bytes_accessed=2 * total * total,
            transcendentals=0,
        ),
        name="backward",
    )(low, grad, delta, query, key, value)


def swap(values, axis, size, bit):
    return lax.ppermute(values, axis, [(i, i ^ bit) for i in range(size)])


def total_over(values, axis, size):
    bit = 1
    while bit < size:
        values = values + swap(values, axis, size, bit)
        bit *= 2
    return values


def move(values, z_step=0, y_step=0, core_step=0):
    pairs = []
    for i in range(16):
        z, y, core = i // 4, i // 2 % 2, i % 2
        pairs.append((i, ((z + z_step) % 4 * 2 + (y ^ y_step)) * 2 + (core ^ core_step)))
    return lax.ppermute(values, "seq", pairs)


def shards(
    queries, key_rows, value_rows, cotangent, attn_gate, lengths, w_out, row_moment, col_moment
):
    seq_size = lax.axis_size("seq")
    dp_size = lax.axis_size("dp")
    inner_dim = queries.shape[2]
    width_dim = cotangent.shape[2]
    columns = width_dim // dp_size
    tokens = queries.shape[1]
    half = tokens // 2
    gate = attn_gate[0][None, :]

    own = cotangent[0]
    side = move(own, y_step=1)
    below, above = move(own, z_step=1), move(own, z_step=3)
    packed = split_columns([queries[0], key_rows[0], value_rows[0]])
    packed = lax.all_to_all(packed, "seq", 0, 0, tiled=True)
    far_low, far_high = move(below[:half], z_step=1), move(above[half:], z_step=3)
    side_below, side_above = move(side, z_step=1), move(side, z_step=3)
    packed, side, below, above, far_low, far_high, side_below, side_above = lax.optimization_barrier(
        (packed, side, below, above, far_low, far_high, side_below, side_above)
    )
    side_low, side_high = move(far_low, y_step=1), move(far_high, y_step=1)
    found = [
        (own, 0, 0, 0),
        (side, 0, 1, 0),
        (below, 3, 0, 0),
        (above, 1, 0, 0),
        (side_below, 3, 1, 0),
        (side_above, 1, 1, 0),
        (far_low, 2, 0, 0),
        (far_high, 2, 0, half),
        (side_low, 2, 1, 0),
        (side_high, 2, 1, half),
    ]
    me = lax.axis_index("seq")
    z, y, core = me // 4, me // 2 % 2, me % 2
    pieces, places = [], []
    for core_step in range(2):
        for rows, z_step, y_step, offset in found:
            rows = move(rows, core_step=1) if core_step else rows
            device = ((z + z_step) % 4 * 2 + (y ^ y_step)) * 2 + (core ^ core_step)
            pieces.append((rows, len(places)))
            places.append(device * tokens + offset)

    weight = w_out.astype(F32)
    gated = (weight * gate).astype(BF16)
    low, attended, query, inverse, key, value = forward(lengths, packed)
    grad, delta, outer = project(
        jnp.stack(places).astype(jnp.int32), pieces, gated, attended, inverse
    )

    partial = (outer * gate).astype(BF16).reshape(HEAD_DIM, dp_size, columns)
    partial = lax.all_to_all(partial.transpose(1, 0, 2), "dp", 0, 0, tiled=True)
    back = backward(low, grad, delta, query, key, value, seq_size)
    back, partial = lax.optimization_barrier((back, partial))
    back = lax.all_to_all(back, "seq", 0, 0, tiled=True)

    grad_weight = jnp.sum(partial.astype(F32), axis=0)
    squares = grad_weight * grad_weight + EPSILON
    gate_part = jnp.sum(weight * outer, axis=0)
    row_total = total_over(jnp.sum(squares, axis=1), "dp", dp_size)
    joined = jnp.concatenate([jnp.sum(squares, axis=0), gate_part])
    joined = total_over(joined, "seq", seq_size)
    row_new = 0.8 * row_moment + 0.2 * (row_total / width_dim)
    col_new = 0.8 * col_moment + 0.2 * (joined[:columns] / inner_dim)
    grad_q, grad_k, grad_v = join_columns(back)
    return (
        grad_q[None],
        grad_k[None],
        grad_v[None],
        joined[columns:][None],
        grad_weight,
        row_new,
        col_new,
    )


def solution(mesh):
    tokens = P("dp", "seq", None)
    return jax.shard_map(
        shards,
        mesh=mesh,
        in_specs=(
            tokens,
            tokens,
            tokens,
            tokens,
            P("dp", None),
            P("dp"),
            P("seq", None),
            P("seq"),
            P("dp"),
        ),
        out_specs=(
            tokens,
            tokens,
            tokens,
            P("dp", None),
            P("seq", "dp"),
            P("seq"),
            P("dp"),
        ),
        check_vma=False,
    )
```

```python
import jax
import jax.numpy as jnp
from jax import lax
from jax.experimental import pallas as pl
from jax.experimental.pallas import tpu as pltpu
from jax.sharding import PartitionSpec as P

HEAD_DIM = 128
SCALE = 1.0 / HEAD_DIM**0.5
LOG2E = 1.4426950408889634
EPSILON = 1e-30
BLOCK = 512
BF16 = jnp.bfloat16
F32 = jnp.float32
PARAMS = pltpu.CompilerParams(vmem_limit_bytes=56 * 2**20)


def contract(left, right, left_dim, right_dim):
    return lax.dot_general(
        left, right, (((left_dim,), (right_dim,)), ((), ())), preferred_element_type=F32
    )


def split_columns(sources):
    tokens, inner = sources[0].shape
    heads = inner // HEAD_DIM
    count = len(sources)
    block = tokens // 4

    def body(*refs):
        out = refs[count]
        for which in range(count):
            for head in range(heads):
                out[head, which] = refs[which][:, head * HEAD_DIM : (head + 1) * HEAD_DIM]

    return pl.pallas_call(
        body,
        grid=(tokens // block,),
        in_specs=[pl.BlockSpec((block, inner), lambda i: (i, 0))] * count,
        out_specs=pl.BlockSpec((heads, count, block, HEAD_DIM), lambda i: (0, 0, i, 0)),
        out_shape=jax.ShapeDtypeStruct((heads, count, tokens, HEAD_DIM), BF16),
        name="split_columns",
    )(*sources)


def join_columns(stacked):
    heads, count, tokens, _ = stacked.shape
    inner = heads * HEAD_DIM
    block = tokens // 4

    def body(*refs):
        rows = pl.ds(pl.program_id(0) * block, block)
        for which in range(count):
            for head in range(heads):
                refs[1 + which][:, head * HEAD_DIM : (head + 1) * HEAD_DIM] = refs[0][
                    head, which, rows, :
                ]

    return pl.pallas_call(
        body,
        grid=(tokens // block,),
        in_specs=[pl.BlockSpec(memory_space=pltpu.VMEM)],
        out_specs=[pl.BlockSpec((block, inner), lambda i: (i, 0))] * count,
        out_shape=[jax.ShapeDtypeStruct((tokens, inner), BF16)] * count,
        compiler_params=pltpu.CompilerParams(vmem_limit_bytes=12 * 2**20),
        name="join_columns",
    )(stacked)


def forward(valid_len, packed):
    parts, _, tokens, _ = packed.shape
    total = parts * tokens
    span = BLOCK // tokens
    steps = total // BLOCK
    chunk = 512

    def body(
        len_ref, p_ref, e_ref, att_ref, qt_ref, inv_ref, kt_ref, va_ref, ka, vt, held, tops
    ):
        step = pl.program_id(0)
        length = len_ref[0]

        @pl.when(step == 0)
        def _():
            key_rows = p_ref[:, 1].reshape(total, HEAD_DIM)
            value_rows = p_ref[:, 2].reshape(total, HEAD_DIM)
            row = lax.broadcasted_iota(jnp.int32, (total, HEAD_DIM), 0)
            col = lax.broadcasted_iota(jnp.int32, (total, HEAD_DIM), 1)
            ka[:, :HEAD_DIM] = key_rows
            ka[:, HEAD_DIM:] = jnp.where((row >= length) & (col == 0), -1e30, 0.0).astype(BF16)
            vt[:HEAD_DIM, :] = value_rows.T
            vt[HEAD_DIM:, :] = jnp.ones((16, total), BF16)
            kt_ref[...] = key_rows.T
            va_ref[:, :HEAD_DIM] = value_rows
            va_ref[:, HEAD_DIM:] = jnp.where(col < 2, 1.0, 0.0).astype(BF16)

        def live(block):
            slot = block * BLOCK + lax.broadcasted_iota(jnp.int32, (1, BLOCK), 1)
            return slot < length

        def work(score_next, weigh_last):
            if score_next:
                query = p_ref[pl.ds(step * span, span), 0]
                query = query.reshape(BLOCK, HEAD_DIM).T
                qt_ref[...] = query
                row = lax.broadcasted_iota(jnp.int32, (HEAD_DIM, BLOCK), 0)
                extra = jnp.where(row == 0, 1.0, 0.0).astype(BF16)
                widened = jnp.concatenate([query, extra], axis=0)
                top = jnp.full((8, BLOCK), -3e38, F32)
            if weigh_last:
                shift = tops[0:1]
                summed = jnp.zeros((HEAD_DIM + 16, BLOCK), F32)
            for first in range(0, total, chunk):
                rows = slice(first, first + chunk)
                if weigh_last:
                    low = jnp.exp2(held[rows, :] * (SCALE * LOG2E) - shift).astype(BF16)
                    e_ref[rows, :] = low
                if score_next:
                    scores = contract(ka[rows, :], widened, 1, 0)
                    held[rows, :] = scores
                    top = jnp.maximum(top, jnp.max(scores.reshape(chunk // 8, 8, BLOCK), axis=0))
                if weigh_last:
                    summed = summed + contract(vt[:, rows], low, 1, 0)
            if weigh_last:
                inverse = jnp.where(live(step - 1), 1.0 / summed[HEAD_DIM : HEAD_DIM + 1], 0.0)
                att_ref[...] = (summed[:HEAD_DIM] * inverse).astype(BF16)
                inv_ref[...] = jnp.broadcast_to(inverse, (8, BLOCK))
            if score_next:
                top = jnp.max(top, axis=0, keepdims=True) * (SCALE * LOG2E)
                tops[...] = jnp.broadcast_to(jnp.where(live(step), top, 1e30), (8, BLOCK))

        pl.when(step == 0)(lambda: work(True, False))
        pl.when((step > 0) & (step < steps))(lambda: work(True, True))
        pl.when(step == steps)(lambda: work(False, True))

    whole = lambda i, n: (0, 0)
    scored = lambda i, n: (0, jnp.minimum(i, steps - 1))
    weighed = lambda i, n: (0, jnp.maximum(i - 1, 0))
    return pl.pallas_call(
        body,
        grid_spec=pltpu.PrefetchScalarGridSpec(
            num_scalar_prefetch=1,
            grid=(steps + 1,),
            in_specs=[
                pl.BlockSpec(memory_space=pltpu.VMEM),
            ],
            out_specs=[
                pl.BlockSpec((total, BLOCK), weighed),
                pl.BlockSpec((HEAD_DIM, BLOCK), weighed),
                pl.BlockSpec((HEAD_DIM, BLOCK), scored),
                pl.BlockSpec((8, BLOCK), weighed),
                pl.BlockSpec((HEAD_DIM, total), whole),
                pl.BlockSpec((total, 2 * HEAD_DIM), whole),
            ],
            scratch_shapes=[
                pltpu.VMEM((total, 2 * HEAD_DIM), BF16),
                pltpu.VMEM((HEAD_DIM + 16, total), BF16),
                pltpu.VMEM((total, BLOCK), F32),
                pltpu.VMEM((8, BLOCK), F32),
            ],
        ),
        out_shape=[
            jax.ShapeDtypeStruct((total, total), BF16),
            jax.ShapeDtypeStruct((HEAD_DIM, total), BF16),
            jax.ShapeDtypeStruct((HEAD_DIM, total), BF16),
            jax.ShapeDtypeStruct((8, total), F32),
            jax.ShapeDtypeStruct((HEAD_DIM, total), BF16),
            jax.ShapeDtypeStruct((total, 2 * HEAD_DIM), BF16),
        ],
        compiler_params=pltpu.CompilerParams(vmem_limit_bytes=40 * 2**20),
        cost_estimate=pl.CostEstimate(
            flops=6 * total * total * HEAD_DIM,
            bytes_accessed=2 * total * total,
            transcendentals=total * total,
        ),
        name="forward",
    )(valid_len, packed)


def project(places, pieces, gated, attended, inverse, earlier):
    width = gated.shape[1]
    total = attended.shape[1]
    count = len(pieces)
    sizes = [piece.shape[0] for piece in pieces]
    starts = [sum(sizes[:i]) for i in range(count)]
    groups, filled = [[]], 0
    for i in range(count):
        if filled == 1024:
            groups.append([])
            filled = 0
        groups[-1].append(i)
        filled += sizes[i]

    def body(*refs):
        place_ref, sources = refs[0], refs[1 : 1 + count]
        w_ref, o_ref, inv_ref = refs[1 + count : 4 + count]
        before = refs[4 + count : 4 + count + len(earlier)]
        g_ref, d_ref, a_ref, held, sems = refs[4 + count + len(earlier) :]
        copies = [
            pltpu.make_async_copy(
                sources[i], held.at[pl.ds(starts[i], sizes[i]), :], sems.at[i]
            )
            for i in range(count)
        ]
        for copy in copies:
            copy.start()
        outer = jnp.zeros((HEAD_DIM, width), F32)
        if before:
            g_ref[...] = before[0][...]
            d_ref[...] = before[1][...]
            outer = before[2][...]
        for group in groups:
            lanes = [
                pl.ds(pl.multiple_of(place_ref[i], HEAD_DIM), sizes[i]) for i in group
            ]
            out = jnp.concatenate([o_ref[:, lane] for lane in lanes], axis=1)
            inv = jnp.concatenate([inv_ref[0:1, lane] for lane in lanes], axis=1)
            for i in group:
                copies[i].wait()
            first, last = group[0], group[-1]
            rows = held[starts[first] : starts[last] + sizes[last], :]
            grad = contract(w_ref[...], rows, 1, 1).astype(BF16).astype(F32)
            low = (grad * inv).astype(BF16)
            delta = jnp.sum(low.astype(F32) * out.astype(F32), axis=0, keepdims=True)
            for i, lane in zip(group, lanes):
                at = slice(starts[i] - starts[first], starts[i] - starts[first] + sizes[i])
                g_ref[:, lane] = low[:, at]
                d_ref[:, lane] = jnp.broadcast_to(delta[:, at], (8, sizes[i]))
            outer = outer + contract(out, rows, 1, 0)
        a_ref[...] = outer

    vmem = pl.BlockSpec(memory_space=pltpu.VMEM)
    return pl.pallas_call(
        body,
        in_specs=[pl.BlockSpec(memory_space=pltpu.SMEM)]
        + [pl.BlockSpec(memory_space=pl.ANY)] * count
        + [vmem] * (3 + len(earlier)),
        out_specs=[vmem] * 3,
        out_shape=[
            jax.ShapeDtypeStruct((HEAD_DIM, total), BF16),
            jax.ShapeDtypeStruct((8, total), F32),
            jax.ShapeDtypeStruct((HEAD_DIM, width), F32),
        ],
        scratch_shapes=[
            pltpu.VMEM((sum(sizes), width), BF16),
            pltpu.SemaphoreType.DMA((count,)),
        ],
        compiler_params=PARAMS,
        cost_estimate=pl.CostEstimate(
            flops=4 * sum(sizes) * width * HEAD_DIM,
            bytes_accessed=2 * sum(sizes) * width,
            transcendentals=0,
        ),
        name="project",
    )(places, *pieces, gated, attended, inverse, *earlier)


def backward(low, grad, delta, query, key, value, parts):
    total = low.shape[0]
    tokens = total // parts
    span = BLOCK // tokens
    steps = total // BLOCK
    chunk = 1024

    def body(e_ref, g_ref, d_ref, q_ref, k_ref, v_ref, o_ref, dk, dv):
        step = pl.program_id(0)

        @pl.when(step == 0)
        def _():
            dk[...] = jnp.zeros_like(dk)
            dv[...] = jnp.zeros_like(dv)

        minus = -d_ref[0:1]
        high = minus.astype(BF16).astype(F32)
        row = lax.broadcasted_iota(jnp.int32, (HEAD_DIM, BLOCK), 0)
        extra = jnp.where(row == 0, high, jnp.where(row == 1, minus - high, 0.0)).astype(BF16)
        grad_block = g_ref[...]
        widened = jnp.concatenate([grad_block, extra], axis=0)
        grad_rows = grad_block.T
        query_rows = q_ref[...].T
        dq = jnp.zeros((HEAD_DIM, BLOCK), F32)
        for first in range(0, total, chunk):
            rows = slice(first, first + chunk)
            dprob = contract(v_ref[rows, :], widened, 1, 0)
            probs = e_ref[rows, :]
            dscore = (probs.astype(F32) * dprob).astype(BF16)
            dq = dq + contract(k_ref[:, rows], dscore, 1, 0)
            dv[rows, :] += contract(probs, grad_rows, 1, 0)
            dk[rows, :] += contract(dscore, query_rows, 1, 0)
        dq = (dq * SCALE).T.astype(BF16).reshape(span, tokens, HEAD_DIM)
        o_ref[pl.ds(step * span, span), 0] = dq

        @pl.when(step == steps - 1)
        def _():
            o_ref[:, 1] = (dk[...] * SCALE).astype(BF16).reshape(parts, tokens, HEAD_DIM)
            o_ref[:, 2] = dv[...].astype(BF16).reshape(parts, tokens, HEAD_DIM)

    column = lambda i: (0, i)
    whole = lambda i: (0, 0)
    return pl.pallas_call(
        body,
        grid=(steps,),
        in_specs=[
            pl.BlockSpec((total, BLOCK), column),
            pl.BlockSpec((HEAD_DIM, BLOCK), column),
            pl.BlockSpec((8, BLOCK), column),
            pl.BlockSpec((HEAD_DIM, BLOCK), column),
            pl.BlockSpec((HEAD_DIM, total), whole),
            pl.BlockSpec((total, 2 * HEAD_DIM), whole),
        ],
        out_specs=pl.BlockSpec((parts, 3, tokens, HEAD_DIM), lambda i: (0, 0, 0, 0)),
        out_shape=jax.ShapeDtypeStruct((parts, 3, tokens, HEAD_DIM), BF16),
        scratch_shapes=[pltpu.VMEM((total, HEAD_DIM), F32)] * 2,
        compiler_params=PARAMS,
        cost_estimate=pl.CostEstimate(
            flops=10 * total * total * HEAD_DIM,
            bytes_accessed=2 * total * total,
            transcendentals=0,
        ),
        name="backward",
    )(low, grad, delta, query, key, value)


def swap(values, axis, size, bit):
    return lax.ppermute(values, axis, [(i, i ^ bit) for i in range(size)])


def total_over(values, axis, size):
    bit = 1
    while bit < size:
        values = values + swap(values, axis, size, bit)
        bit *= 2
    return values


def move(values, z_step=0, y_step=0, core_step=0):
    pairs = []
    for i in range(16):
        z, y, core = i // 4, i // 2 % 2, i % 2
        pairs.append((i, ((z + z_step) % 4 * 2 + (y ^ y_step)) * 2 + (core ^ core_step)))
    return lax.ppermute(values, "seq", pairs)


def shards(
    queries, key_rows, value_rows, cotangent, attn_gate, lengths, w_out, row_moment, col_moment
):
    seq_size = lax.axis_size("seq")
    dp_size = lax.axis_size("dp")
    inner_dim = queries.shape[2]
    width_dim = cotangent.shape[2]
    columns = width_dim // dp_size
    tokens = queries.shape[1]
    half = tokens // 2
    gate = attn_gate[0][None, :]

    own = cotangent[0]
    side = move(own, y_step=1)
    below, above = move(own, z_step=1), move(own, z_step=3)
    packed = split_columns([queries[0], key_rows[0], value_rows[0]])
    packed, side, below, above = lax.optimization_barrier((packed, side, below, above))
    packed = lax.all_to_all(packed, "seq", 0, 0, tiled=True)
    far_low, far_high = move(below[:half], z_step=1), move(above[half:], z_step=3)
    side_below, side_above = move(side, z_step=1), move(side, z_step=3)
    side_low, side_high = move(far_low, y_step=1), move(far_high, y_step=1)
    found = [
        (own, 0, 0, 0),
        (side, 0, 1, 0),
        (below, 3, 0, 0),
        (above, 1, 0, 0),
        (far_low, 2, 0, 0),
        (far_high, 2, 0, half),
        (side_below, 3, 1, 0),
        (side_above, 1, 1, 0),
        (side_low, 2, 1, 0),
        (side_high, 2, 1, half),
    ]
    me = lax.axis_index("seq")
    z, y, core = me // 4, me // 2 % 2, me % 2

    weight = w_out.astype(F32)
    gated = (weight * gate).astype(BF16)
    low, attended, query, inverse, key, value = forward(lengths, packed)
    made = []
    for some in (found[:8], found[8:]):
        pieces, places = [], []
        for core_step in range(2):
            for rows, z_step, y_step, offset in some:
                device = ((z + z_step) % 4 * 2 + (y ^ y_step)) * 2 + (core ^ core_step)
                pieces.append(move(rows, core_step=1) if core_step else rows)
                places.append(device * tokens + offset)
        made = project(
            jnp.stack(places).astype(jnp.int32), pieces, gated, attended, inverse, made
        )
    grad, delta, outer = made

    partial = (outer * gate).astype(BF16).reshape(HEAD_DIM, dp_size, columns)
    partial = lax.all_to_all(partial.transpose(1, 0, 2), "dp", 0, 0, tiled=True)
    back = backward(low, grad, delta, query, key, value, seq_size)
    back, partial = lax.optimization_barrier((back, partial))
    back = lax.all_to_all(back, "seq", 0, 0, tiled=True)

    grad_weight = jnp.sum(partial.astype(F32), axis=0)
    squares = grad_weight * grad_weight + EPSILON
    gate_part = jnp.sum(weight * outer, axis=0)
    row_total = total_over(jnp.sum(squares, axis=1), "dp", dp_size)
    joined = jnp.concatenate([jnp.sum(squares, axis=0), gate_part])
    joined = total_over(joined, "seq", seq_size)
    row_new = 0.8 * row_moment + 0.2 * (row_total / width_dim)
    col_new = 0.8 * col_moment + 0.2 * (joined[:columns] / inner_dim)
    grad_q, grad_k, grad_v = join_columns(back)
    return (
        grad_q[None],
        grad_k[None],
        grad_v[None],
        joined[columns:][None],
        grad_weight,
        row_new,
        col_new,
    )


def solution(mesh):
    tokens = P("dp", "seq", None)
    return jax.shard_map(
        shards,
        mesh=mesh,
        in_specs=(
            tokens,
            tokens,
            tokens,
            tokens,
            P("dp", None),
            P("dp"),
            P("seq", None),
            P("seq"),
            P("dp"),
        ),
        out_specs=(
            tokens,
            tokens,
            tokens,
            P("dp", None),
            P("seq", "dp"),
            P("seq"),
            P("dp"),
        ),
        check_vma=False,
    )
```

```python
import jax
import jax.numpy as jnp
from jax import lax
from jax.experimental import pallas as pl
from jax.experimental.pallas import tpu as pltpu
from jax.sharding import PartitionSpec as P

HEAD_DIM = 128
SCALE = 1.0 / HEAD_DIM**0.5
LOG2E = 1.4426950408889634
EPSILON = 1e-30
BLOCK = 512
BF16 = jnp.bfloat16
F32 = jnp.float32
PARAMS = pltpu.CompilerParams(vmem_limit_bytes=56 * 2**20)


def contract(left, right, left_dim, right_dim):
    return lax.dot_general(
        left, right, (((left_dim,), (right_dim,)), ((), ())), preferred_element_type=F32
    )


def split_columns(sources):
    tokens, inner = sources[0].shape
    heads = inner // HEAD_DIM
    count = len(sources)
    block = tokens // 4

    def body(*refs):
        out = refs[count]
        for which in range(count):
            for head in range(heads):
                out[head, which] = refs[which][:, head * HEAD_DIM : (head + 1) * HEAD_DIM]

    return pl.pallas_call(
        body,
        grid=(tokens // block,),
        in_specs=[pl.BlockSpec((block, inner), lambda i: (i, 0))] * count,
        out_specs=pl.BlockSpec((heads, count, block, HEAD_DIM), lambda i: (0, 0, i, 0)),
        out_shape=jax.ShapeDtypeStruct((heads, count, tokens, HEAD_DIM), BF16),
        name="split_columns",
    )(*sources)


def join_columns(early, late):
    heads, _, half, _ = early.shape
    inner = heads * HEAD_DIM

    def body(early_ref, late_ref, dq, dk, dv, sums):
        step = pl.program_id(0)
        for head in range(heads):
            lanes = slice(head * HEAD_DIM, (head + 1) * HEAD_DIM)
            dq[:, lanes] = late_ref[head, pl.ds(step * half, half), :]

        @pl.when(step == 0)
        def _():
            for head in range(heads):
                lanes = slice(head * HEAD_DIM, (head + 1) * HEAD_DIM)
                dk[:, lanes] = early_ref[head, 0]
                dv[:, lanes] = early_ref[head, 1]
            total = jnp.zeros((16, HEAD_DIM), F32)
            for head in range(heads):
                total = total + late_ref[head, 4 * half : 4 * half + 16, :].astype(F32)
                total = total + late_ref[head, 4 * half + 16 : 4 * half + 32, :].astype(F32)
            sums[...] = total

        @pl.when(step == 1)
        def _():
            for head in range(heads):
                lanes = slice(head * HEAD_DIM, (head + 1) * HEAD_DIM)
                dk[:, lanes] = late_ref[head, 2 * half : 3 * half, :]
                dv[:, lanes] = late_ref[head, 3 * half : 4 * half, :]

    rows = pl.BlockSpec((half, inner), lambda i: (i, 0))
    return pl.pallas_call(
        body,
        grid=(2,),
        in_specs=[pl.BlockSpec(memory_space=pltpu.VMEM)] * 2,
        out_specs=[rows, rows, rows, pl.BlockSpec((16, HEAD_DIM), lambda i: (0, 0))],
        out_shape=[jax.ShapeDtypeStruct((2 * half, inner), BF16)] * 3
        + [jax.ShapeDtypeStruct((16, HEAD_DIM), F32)],
        compiler_params=pltpu.CompilerParams(vmem_limit_bytes=16 * 2**20),
        name="join_columns",
    )(early, late)


def forward(valid_len, packed):
    parts, _, tokens, _ = packed.shape
    total = parts * tokens
    span = BLOCK // tokens
    steps = total // BLOCK
    chunk = 512

    def body(
        len_ref, p_ref, e_ref, att_ref, qt_ref, inv_ref, kt_ref, va_ref, ka, vt, held, tops
    ):
        step = pl.program_id(0)
        length = len_ref[0]

        @pl.when(step == 0)
        def _():
            half = tokens // 2
            some = total // 2
            row = lax.broadcasted_iota(jnp.int32, (some, HEAD_DIM), 0)
            col = lax.broadcasted_iota(jnp.int32, (some, HEAD_DIM), 1)
            vt[HEAD_DIM:, :] = jnp.ones((16, total), BF16)
            for part in range(2):
                of = slice(part * half, (part + 1) * half)
                at = slice(part * some, (part + 1) * some)
                key_rows = p_ref[:, 1, of, :].reshape(some, HEAD_DIM)
                value_rows = p_ref[:, 2, of, :].reshape(some, HEAD_DIM)
                slot = row // half * tokens + part * half + row % half
                ka[at, :HEAD_DIM] = key_rows
                ka[at, HEAD_DIM:] = jnp.where((slot >= length) & (col == 0), -1e30, 0.0).astype(
                    BF16
                )
                vt[:HEAD_DIM, at] = value_rows.T
                kt_ref[:, at] = key_rows.T
                va_ref[at, :HEAD_DIM] = value_rows
                va_ref[at, HEAD_DIM:] = jnp.where(col < 2, 1.0, 0.0).astype(BF16)

        def live(block):
            slot = block * BLOCK + lax.broadcasted_iota(jnp.int32, (1, BLOCK), 1)
            return slot < length

        def work(score_next, weigh_last):
            if score_next:
                query = p_ref[pl.ds(step * span, span), 0]
                query = query.reshape(BLOCK, HEAD_DIM).T
                qt_ref[...] = query
                row = lax.broadcasted_iota(jnp.int32, (HEAD_DIM, BLOCK), 0)
                extra = jnp.where(row == 0, 1.0, 0.0).astype(BF16)
                widened = jnp.concatenate([query, extra], axis=0)
                top = jnp.full((8, BLOCK), -3e38, F32)
            if weigh_last:
                shift = tops[0:1]
                summed = jnp.zeros((HEAD_DIM + 16, BLOCK), F32)
            for first in range(0, total, chunk):
                rows = slice(first, first + chunk)
                if weigh_last:
                    low = jnp.exp2(held[rows, :] * (SCALE * LOG2E) - shift).astype(BF16)
                    e_ref[rows, :] = low
                if score_next:
                    scores = contract(ka[rows, :], widened, 1, 0)
                    held[rows, :] = scores
                    top = jnp.maximum(top, jnp.max(scores.reshape(chunk // 8, 8, BLOCK), axis=0))
                if weigh_last:
                    summed = summed + contract(vt[:, rows], low, 1, 0)
            if weigh_last:
                inverse = jnp.where(live(step - 1), 1.0 / summed[HEAD_DIM : HEAD_DIM + 1], 0.0)
                att_ref[...] = (summed[:HEAD_DIM] * inverse).astype(BF16)
                inv_ref[...] = jnp.broadcast_to(inverse, (8, BLOCK))
            if score_next:
                top = jnp.max(top, axis=0, keepdims=True) * (SCALE * LOG2E)
                tops[...] = jnp.broadcast_to(jnp.where(live(step), top, 1e30), (8, BLOCK))

        pl.when(step == 0)(lambda: work(True, False))
        pl.when((step > 0) & (step < steps))(lambda: work(True, True))
        pl.when(step == steps)(lambda: work(False, True))

    whole = lambda i, n: (0, 0)
    scored = lambda i, n: (0, jnp.minimum(i, steps - 1))
    weighed = lambda i, n: (0, jnp.maximum(i - 1, 0))
    return pl.pallas_call(
        body,
        grid_spec=pltpu.PrefetchScalarGridSpec(
            num_scalar_prefetch=1,
            grid=(steps + 1,),
            in_specs=[
                pl.BlockSpec(memory_space=pltpu.VMEM),
            ],
            out_specs=[
                pl.BlockSpec((total, BLOCK), weighed),
                pl.BlockSpec((HEAD_DIM, BLOCK), weighed),
                pl.BlockSpec((HEAD_DIM, BLOCK), scored),
                pl.BlockSpec((8, BLOCK), weighed),
                pl.BlockSpec((HEAD_DIM, total), whole),
                pl.BlockSpec((total, 2 * HEAD_DIM), whole),
            ],
            scratch_shapes=[
                pltpu.VMEM((total, 2 * HEAD_DIM), BF16),
                pltpu.VMEM((HEAD_DIM + 16, total), BF16),
                pltpu.VMEM((total, BLOCK), F32),
                pltpu.VMEM((8, BLOCK), F32),
            ],
        ),
        out_shape=[
            jax.ShapeDtypeStruct((total, total), BF16),
            jax.ShapeDtypeStruct((HEAD_DIM, total), BF16),
            jax.ShapeDtypeStruct((HEAD_DIM, total), BF16),
            jax.ShapeDtypeStruct((8, total), F32),
            jax.ShapeDtypeStruct((HEAD_DIM, total), BF16),
            jax.ShapeDtypeStruct((total, 2 * HEAD_DIM), BF16),
        ],
        compiler_params=pltpu.CompilerParams(vmem_limit_bytes=40 * 2**20),
        cost_estimate=pl.CostEstimate(
            flops=6 * total * total * HEAD_DIM,
            bytes_accessed=2 * total * total,
            transcendentals=total * total,
        ),
        name="forward",
    )(valid_len, packed)


def project(places, pieces, gated, attended, inverse, earlier):
    width = gated.shape[1]
    total = attended.shape[1]
    count = len(pieces)
    sizes = [piece.shape[0] for piece in pieces]
    starts = [sum(sizes[:i]) for i in range(count)]
    groups, filled = [[]], 0
    for i in range(count):
        if filled == 1024:
            groups.append([])
            filled = 0
        groups[-1].append(i)
        filled += sizes[i]

    def body(*refs):
        place_ref, sources = refs[0], refs[1 : 1 + count]
        w_ref, o_ref, inv_ref = refs[1 + count : 4 + count]
        before = refs[4 + count : 4 + count + len(earlier)]
        g_ref, d_ref, a_ref, held, sems = refs[4 + count + len(earlier) :]
        copies = [
            pltpu.make_async_copy(
                sources[i], held.at[pl.ds(starts[i], sizes[i]), :], sems.at[i]
            )
            for i in range(count)
        ]
        for copy in copies:
            copy.start()
        outer = jnp.zeros((HEAD_DIM, width), F32)
        if before:
            g_ref[...] = before[0][...]
            d_ref[...] = before[1][...]
            outer = before[2][...]
        for group in groups:
            lanes = [
                pl.ds(pl.multiple_of(place_ref[i], HEAD_DIM), sizes[i]) for i in group
            ]
            out = jnp.concatenate([o_ref[:, lane] for lane in lanes], axis=1)
            inv = jnp.concatenate([inv_ref[0:1, lane] for lane in lanes], axis=1)
            for i in group:
                copies[i].wait()
            first, last = group[0], group[-1]
            rows = held[starts[first] : starts[last] + sizes[last], :]
            grad = contract(w_ref[...], rows, 1, 1).astype(BF16).astype(F32)
            low = (grad * inv).astype(BF16)
            delta = jnp.sum(low.astype(F32) * out.astype(F32), axis=0, keepdims=True)
            for i, lane in zip(group, lanes):
                at = slice(starts[i] - starts[first], starts[i] - starts[first] + sizes[i])
                g_ref[:, lane] = low[:, at]
                d_ref[:, lane] = jnp.broadcast_to(delta[:, at], (8, sizes[i]))
            outer = outer + contract(out, rows, 1, 0)
        a_ref[...] = outer

    vmem = pl.BlockSpec(memory_space=pltpu.VMEM)
    return pl.pallas_call(
        body,
        in_specs=[pl.BlockSpec(memory_space=pltpu.SMEM)]
        + [pl.BlockSpec(memory_space=pl.ANY)] * count
        + [vmem] * (3 + len(earlier)),
        out_specs=[vmem] * 3,
        out_shape=[
            jax.ShapeDtypeStruct((HEAD_DIM, total), BF16),
            jax.ShapeDtypeStruct((8, total), F32),
            jax.ShapeDtypeStruct((HEAD_DIM, width), F32),
        ],
        scratch_shapes=[
            pltpu.VMEM((sum(sizes), width), BF16),
            pltpu.SemaphoreType.DMA((count,)),
        ],
        compiler_params=pltpu.CompilerParams(vmem_limit_bytes=28 * 2**20),
        cost_estimate=pl.CostEstimate(
            flops=4 * sum(sizes) * width * HEAD_DIM,
            bytes_accessed=2 * sum(sizes) * width,
            transcendentals=0,
        ),
        name="project",
    )(places, *pieces, gated, attended, inverse, *earlier)


def backward(which, low, grad, delta, query, key, value, parts, earlier):
    total = low.shape[0]
    half = total // parts // 2
    span = BLOCK // (2 * half)
    steps = total // BLOCK
    some = total // 2
    chunk = 1024

    def body(*refs):
        e_ref, g_ref, d_ref, q_ref, k_ref, v_ref = refs[:6]
        if which:
            dq_ref, extra_ref, o_ref, dk, dv = refs[6:]
        else:
            sum_ref, o_ref, dk, dv = refs[6:]
        step = pl.program_id(0)

        @pl.when(step == 0)
        def _():
            dk[...] = jnp.zeros_like(dk)
            dv[...] = jnp.zeros_like(dv)

        minus = -d_ref[0:1]
        high = minus.astype(BF16).astype(F32)
        row = lax.broadcasted_iota(jnp.int32, (HEAD_DIM, BLOCK), 0)
        extra = jnp.where(row == 0, high, jnp.where(row == 1, minus - high, 0.0)).astype(BF16)
        grad_block = g_ref[...]
        widened = jnp.concatenate([grad_block, extra], axis=0)
        grad_rows = grad_block.T
        query_rows = q_ref[...].T
        dq = dq_ref[...] if which else jnp.zeros((HEAD_DIM, BLOCK), F32)
        for first in range(0, some, chunk):
            rows = slice(first, first + chunk)
            dprob = contract(v_ref[rows, :], widened, 1, 0)
            probs = e_ref[rows, :]
            dscore = (probs.astype(F32) * dprob).astype(BF16)
            dq = dq + contract(k_ref[:, rows], dscore, 1, 0)
            dv[rows, :] += contract(probs, grad_rows, 1, 0)
            dk[rows, :] += contract(dscore, query_rows, 1, 0)
        if which:
            o_ref[pl.ds(step * span, span), : 2 * half, :] = (
                (dq * SCALE).T.astype(BF16).reshape(span, 2 * half, HEAD_DIM)
            )
        else:
            sum_ref[...] = dq

        @pl.when(step == steps - 1)
        def _():
            dk_low = (dk[...] * SCALE).astype(BF16).reshape(parts, half, HEAD_DIM)
            dv_low = dv[...].astype(BF16).reshape(parts, half, HEAD_DIM)
            if which:
                o_ref[:, 2 * half : 3 * half, :] = dk_low
                o_ref[:, 3 * half : 4 * half, :] = dv_low
                vector = extra_ref[...]
                first = vector.astype(BF16)
                rest = (vector - first.astype(F32)).astype(BF16)
                both = jnp.concatenate([first, rest], axis=0)
                o_ref[:, 4 * half :, :] = jnp.broadcast_to(both[None], (parts, 32, HEAD_DIM))
            else:
                o_ref[:, 0] = dk_low
                o_ref[:, 1] = dv_low

    column = lambda i: (0, i)
    shape = (parts, 4 * half + 32, HEAD_DIM) if which else (parts, 2, half, HEAD_DIM)
    out_specs = [pl.BlockSpec(shape, lambda i: (0,) * len(shape))]
    out_shape = [jax.ShapeDtypeStruct(shape, BF16)]
    more = []
    if which:
        more = [
            pl.BlockSpec((HEAD_DIM, BLOCK), column),
            pl.BlockSpec((16, HEAD_DIM), lambda i: (0, 0)),
        ]
    else:
        out_specs = [pl.BlockSpec((HEAD_DIM, BLOCK), column)] + out_specs
        out_shape = [jax.ShapeDtypeStruct((HEAD_DIM, total), F32)] + out_shape
    return pl.pallas_call(
        body,
        grid=(steps,),
        in_specs=[
            pl.BlockSpec((some, BLOCK), lambda i: (which, i)),
            pl.BlockSpec((HEAD_DIM, BLOCK), column),
            pl.BlockSpec((8, BLOCK), column),
            pl.BlockSpec((HEAD_DIM, BLOCK), column),
            pl.BlockSpec((HEAD_DIM, some), lambda i: (0, which)),
            pl.BlockSpec((some, 2 * HEAD_DIM), lambda i: (which, 0)),
        ]
        + more,
        out_specs=out_specs,
        out_shape=out_shape,
        scratch_shapes=[pltpu.VMEM((some, HEAD_DIM), F32)] * 2,
        compiler_params=PARAMS,
        cost_estimate=pl.CostEstimate(
            flops=5 * total * total * HEAD_DIM,
            bytes_accessed=total * total,
            transcendentals=0,
        ),
        name="backward",
    )(low, grad, delta, query, key, value, *earlier)


def swap(values, axis, size, bit):
    return lax.ppermute(values, axis, [(i, i ^ bit) for i in range(size)])


def total_over(values, axis):
    one, two, three = (swap(values, axis, 8, bit) for bit in (1, 2, 3))
    values = (values + one) + (two + three)
    return values + swap(values, axis, 8, 4)


def move(values, z_step=0, y_step=0, core_step=0):
    pairs = []
    for i in range(16):
        z, y, core = i // 4, i // 2 % 2, i % 2
        pairs.append((i, ((z + z_step) % 4 * 2 + (y ^ y_step)) * 2 + (core ^ core_step)))
    return lax.ppermute(values, "seq", pairs)


def shards(
    queries, key_rows, value_rows, cotangent, attn_gate, lengths, w_out, row_moment, col_moment
):
    seq_size = lax.axis_size("seq")
    dp_size = lax.axis_size("dp")
    inner_dim = queries.shape[2]
    width_dim = cotangent.shape[2]
    columns = width_dim // dp_size
    tokens = queries.shape[1]
    half = tokens // 2
    gate = attn_gate[0][None, :]

    own = cotangent[0]
    side = move(own, y_step=1)
    below, above = move(own, z_step=1), move(own, z_step=3)
    packed = split_columns([queries[0], key_rows[0], value_rows[0]])
    packed, side, below, above = lax.optimization_barrier((packed, side, below, above))
    packed = lax.all_to_all(packed, "seq", 0, 0, tiled=True)
    far_low, far_high = move(below[:half], z_step=1), move(above[half:], z_step=3)
    side_below, side_above = move(side, z_step=1), move(side, z_step=3)

    weight = w_out.astype(F32)
    gated = (weight * gate).astype(BF16)
    results = forward(lengths, packed)
    results, far_low, far_high, side_below, side_above = lax.optimization_barrier(
        (results, far_low, far_high, side_below, side_above)
    )
    low, attended, query, inverse, key, value = results
    side_low, side_high = move(side_below[:half], z_step=1), move(side_above[half:], z_step=3)
    found = [
        (own, 0, 0, 0),
        (side, 0, 1, 0),
        (below, 3, 0, 0),
        (above, 1, 0, 0),
        (far_low, 2, 0, 0),
        (far_high, 2, 0, half),
        (side_below, 3, 1, 0),
        (side_above, 1, 1, 0),
        (side_low, 2, 1, 0),
        (side_high, 2, 1, half),
    ]
    me = lax.axis_index("seq")
    z, y, core = me // 4, me // 2 % 2, me % 2
    made = []
    for some in (found[:4], found[4:]):
        pieces, places = [], []
        for core_step in range(2):
            for rows, z_step, y_step, offset in some:
                device = ((z + z_step) % 4 * 2 + (y ^ y_step)) * 2 + (core ^ core_step)
                pieces.append(move(rows, core_step=1) if core_step else rows)
                places.append(device * tokens + offset)
        made = project(
            jnp.stack(places).astype(jnp.int32), pieces, gated, attended, inverse, made
        )
    grad, delta, outer = made

    partial = (outer * gate).astype(BF16).reshape(HEAD_DIM, dp_size, columns)
    partial = lax.all_to_all(partial.transpose(1, 0, 2), "dp", 0, 0, tiled=True)
    some_q, early = backward(0, low, grad, delta, query, key, value, seq_size, [])
    some_q, early, partial = lax.optimization_barrier((some_q, early, partial))
    early = lax.all_to_all(early, "seq", 0, 0, tiled=True)
    grad_weight = jnp.sum(partial.astype(F32), axis=0)
    squares = grad_weight * grad_weight + EPSILON
    gate_part = jnp.sum(weight * outer, axis=0)
    row_total = total_over(jnp.sum(squares, axis=1), "dp")
    joined = jnp.concatenate(
        [gate_part, jnp.sum(squares, axis=0), jnp.zeros((320,), F32)]
    ).reshape(16, HEAD_DIM)
    (late,) = backward(
        1, low, grad, delta, query, key, value, seq_size, [some_q, joined]
    )
    early, late = lax.optimization_barrier((early, late))
    late = lax.all_to_all(late, "seq", 0, 0, tiled=True)
    grad_q, grad_k, grad_v, joined = join_columns(early, late)
    joined = joined.reshape(2048)
    row_new = 0.8 * row_moment + 0.2 * (row_total / width_dim)
    col_new = 0.8 * col_moment + 0.2 * (joined[width_dim : width_dim + columns] / inner_dim)
    return (
        grad_q[None],
        grad_k[None],
        grad_v[None],
        joined[:width_dim][None],
        grad_weight,
        row_new,
        col_new,
    )


def solution(mesh):
    tokens = P("dp", "seq", None)
    return jax.shard_map(
        shards,
        mesh=mesh,
        in_specs=(
            tokens,
            tokens,
            tokens,
            tokens,
            P("dp", None),
            P("dp"),
            P("seq", None),
            P("seq"),
            P("dp"),
        ),
        out_specs=(
            tokens,
            tokens,
            tokens,
            P("dp", None),
            P("seq", "dp"),
            P("seq"),
            P("dp"),
        ),
        check_vma=False,
    )
```

```python
import jax
import jax.numpy as jnp
from jax import lax
from jax.experimental import pallas as pl
from jax.experimental.pallas import tpu as pltpu
from jax.sharding import PartitionSpec as P

HEAD_DIM = 128
SCALE = 1.0 / HEAD_DIM**0.5
LOG2E = 1.4426950408889634
EPSILON = 1e-30
BLOCK = 512
BF16 = jnp.bfloat16
F32 = jnp.float32
PARAMS = pltpu.CompilerParams(vmem_limit_bytes=56 * 2**20)


def contract(left, right, left_dim, right_dim):
    return lax.dot_general(
        left, right, (((left_dim,), (right_dim,)), ((), ())), preferred_element_type=F32
    )


def split_columns(sources):
    tokens, inner = sources[0].shape
    heads = inner // HEAD_DIM
    count = len(sources)
    block = tokens // 4

    def body(*refs):
        out = refs[count]
        for which in range(count):
            for head in range(heads):
                out[head, which] = refs[which][:, head * HEAD_DIM : (head + 1) * HEAD_DIM]

    return pl.pallas_call(
        body,
        grid=(tokens // block,),
        in_specs=[pl.BlockSpec((block, inner), lambda i: (i, 0))] * count,
        out_specs=pl.BlockSpec((heads, count, block, HEAD_DIM), lambda i: (0, 0, i, 0)),
        out_shape=jax.ShapeDtypeStruct((heads, count, tokens, HEAD_DIM), BF16),
        name="split_columns",
    )(*sources)


def join_columns(early, late):
    heads, _, half, _ = early.shape
    inner = heads * HEAD_DIM

    def body(early_ref, late_ref, dq, dk, dv, sums):
        step = pl.program_id(0)
        for head in range(heads):
            lanes = slice(head * HEAD_DIM, (head + 1) * HEAD_DIM)
            dq[:, lanes] = late_ref[head, pl.ds(step * half, half), :]

        @pl.when(step == 0)
        def _():
            for head in range(heads):
                lanes = slice(head * HEAD_DIM, (head + 1) * HEAD_DIM)
                dk[:, lanes] = early_ref[head, 0]
                dv[:, lanes] = early_ref[head, 1]
            total = jnp.zeros((16, HEAD_DIM), F32)
            for head in range(heads):
                total = total + late_ref[head, 4 * half : 4 * half + 16, :].astype(F32)
                total = total + late_ref[head, 4 * half + 16 : 4 * half + 32, :].astype(F32)
            sums[...] = total

        @pl.when(step == 1)
        def _():
            for head in range(heads):
                lanes = slice(head * HEAD_DIM, (head + 1) * HEAD_DIM)
                dk[:, lanes] = late_ref[head, 2 * half : 3 * half, :]
                dv[:, lanes] = late_ref[head, 3 * half : 4 * half, :]

    rows = pl.BlockSpec((half, inner), lambda i: (i, 0))
    return pl.pallas_call(
        body,
        grid=(2,),
        in_specs=[pl.BlockSpec(memory_space=pltpu.VMEM)] * 2,
        out_specs=[rows, rows, rows, pl.BlockSpec((16, HEAD_DIM), lambda i: (0, 0))],
        out_shape=[jax.ShapeDtypeStruct((2 * half, inner), BF16)] * 3
        + [jax.ShapeDtypeStruct((16, HEAD_DIM), F32)],
        compiler_params=pltpu.CompilerParams(vmem_limit_bytes=16 * 2**20),
        name="join_columns",
    )(early, late)


def forward(valid_len, packed):
    parts, _, tokens, _ = packed.shape
    total = parts * tokens
    span = BLOCK // tokens
    steps = total // BLOCK
    chunk = 512

    def body(
        len_ref, p_ref, e_ref, att_ref, qt_ref, inv_ref, kt_ref, va_ref, ka, vt, held, tops
    ):
        step = pl.program_id(0)
        length = len_ref[0]

        @pl.when(step == 0)
        def _():
            half = tokens // 2
            some = total // 2
            row = lax.broadcasted_iota(jnp.int32, (some, HEAD_DIM), 0)
            col = lax.broadcasted_iota(jnp.int32, (some, HEAD_DIM), 1)
            vt[HEAD_DIM:, :] = jnp.ones((16, total), BF16)
            for part in range(2):
                of = slice(part * half, (part + 1) * half)
                at = slice(part * some, (part + 1) * some)
                key_rows = p_ref[:, 1, of, :].reshape(some, HEAD_DIM)
                value_rows = p_ref[:, 2, of, :].reshape(some, HEAD_DIM)
                slot = row // half * tokens + part * half + row % half
                ka[at, :HEAD_DIM] = key_rows
                ka[at, HEAD_DIM:] = jnp.where((slot >= length) & (col == 0), -1e30, 0.0).astype(
                    BF16
                )
                vt[:HEAD_DIM, at] = value_rows.T
                kt_ref[:, at] = key_rows.T
                va_ref[at, :HEAD_DIM] = value_rows
                va_ref[at, HEAD_DIM:] = jnp.where(col < 2, 1.0, 0.0).astype(BF16)

        def live(block):
            slot = block * BLOCK + lax.broadcasted_iota(jnp.int32, (1, BLOCK), 1)
            return slot < length

        def work(score_next, weigh_last):
            if score_next:
                query = p_ref[pl.ds(step * span, span), 0]
                query = query.reshape(BLOCK, HEAD_DIM).T
                qt_ref[...] = query
                row = lax.broadcasted_iota(jnp.int32, (HEAD_DIM, BLOCK), 0)
                extra = jnp.where(row == 0, 1.0, 0.0).astype(BF16)
                widened = jnp.concatenate([query, extra], axis=0)
                top = jnp.full((8, BLOCK), -3e38, F32)
            if weigh_last:
                shift = tops[0:1]
                summed = jnp.zeros((HEAD_DIM + 16, BLOCK), F32)
            for first in range(0, total, chunk):
                rows = slice(first, first + chunk)
                if weigh_last:
                    low = jnp.exp2(held[rows, :] * (SCALE * LOG2E) - shift).astype(BF16)
                    e_ref[rows, :] = low
                if score_next:
                    scores = contract(ka[rows, :], widened, 1, 0)
                    held[rows, :] = scores
                    top = jnp.maximum(top, jnp.max(scores.reshape(chunk // 8, 8, BLOCK), axis=0))
                if weigh_last:
                    summed = summed + contract(vt[:, rows], low, 1, 0)
            if weigh_last:
                inverse = jnp.where(live(step - 1), 1.0 / summed[HEAD_DIM : HEAD_DIM + 1], 0.0)
                att_ref[...] = (summed[:HEAD_DIM] * inverse).astype(BF16)
                inv_ref[...] = jnp.broadcast_to(inverse, (8, BLOCK))
            if score_next:
                top = jnp.max(top, axis=0, keepdims=True) * (SCALE * LOG2E)
                tops[...] = jnp.broadcast_to(jnp.where(live(step), top, 1e30), (8, BLOCK))

        pl.when(step == 0)(lambda: work(True, False))
        pl.when((step > 0) & (step < steps))(lambda: work(True, True))
        pl.when(step == steps)(lambda: work(False, True))

    whole = lambda i, n: (0, 0)
    scored = lambda i, n: (0, jnp.minimum(i, steps - 1))
    weighed = lambda i, n: (0, jnp.maximum(i - 1, 0))
    return pl.pallas_call(
        body,
        grid_spec=pltpu.PrefetchScalarGridSpec(
            num_scalar_prefetch=1,
            grid=(steps + 1,),
            in_specs=[
                pl.BlockSpec(memory_space=pltpu.VMEM),
            ],
            out_specs=[
                pl.BlockSpec((total, BLOCK), weighed),
                pl.BlockSpec((HEAD_DIM, BLOCK), weighed),
                pl.BlockSpec((HEAD_DIM, BLOCK), scored),
                pl.BlockSpec((8, BLOCK), weighed),
                pl.BlockSpec((HEAD_DIM, total), whole),
                pl.BlockSpec((total, 2 * HEAD_DIM), whole),
            ],
            scratch_shapes=[
                pltpu.VMEM((total, 2 * HEAD_DIM), BF16),
                pltpu.VMEM((HEAD_DIM + 16, total), BF16),
                pltpu.VMEM((total, BLOCK), F32),
                pltpu.VMEM((8, BLOCK), F32),
            ],
        ),
        out_shape=[
            jax.ShapeDtypeStruct((total, total), BF16),
            jax.ShapeDtypeStruct((HEAD_DIM, total), BF16),
            jax.ShapeDtypeStruct((HEAD_DIM, total), BF16),
            jax.ShapeDtypeStruct((8, total), F32),
            jax.ShapeDtypeStruct((HEAD_DIM, total), BF16),
            jax.ShapeDtypeStruct((total, 2 * HEAD_DIM), BF16),
        ],
        compiler_params=pltpu.CompilerParams(vmem_limit_bytes=40 * 2**20),
        cost_estimate=pl.CostEstimate(
            flops=6 * total * total * HEAD_DIM,
            bytes_accessed=2 * total * total,
            transcendentals=total * total,
        ),
        name="forward",
    )(valid_len, packed)


def project(places, pieces, gated, attended, inverse, earlier):
    width = gated.shape[1]
    total = attended.shape[1]
    count = len(pieces)
    sizes = [piece.shape[0] for piece in pieces]
    starts = [sum(sizes[:i]) for i in range(count)]
    groups, filled = [[]], 0
    for i in range(count):
        if filled == 1024:
            groups.append([])
            filled = 0
        groups[-1].append(i)
        filled += sizes[i]

    def body(*refs):
        place_ref, sources = refs[0], refs[1 : 1 + count]
        w_ref, o_ref, inv_ref = refs[1 + count : 4 + count]
        before = refs[4 + count : 4 + count + len(earlier)]
        g_ref, d_ref, a_ref = refs[4 + count + len(earlier) :]
        outer = jnp.zeros((HEAD_DIM, width), F32)
        if before:
            g_ref[...] = before[0][...]
            d_ref[...] = before[1][...]
            outer = before[2][...]
        for group in groups:
            lanes = [
                pl.ds(pl.multiple_of(place_ref[i], HEAD_DIM), sizes[i]) for i in group
            ]
            out = jnp.concatenate([o_ref[:, lane] for lane in lanes], axis=1)
            inv = jnp.concatenate([inv_ref[0:1, lane] for lane in lanes], axis=1)
            first = group[0]
            rows = jnp.concatenate([sources[i][...] for i in group], axis=0)
            grad = contract(w_ref[...], rows, 1, 1).astype(BF16).astype(F32)
            low = (grad * inv).astype(BF16)
            delta = jnp.sum(low.astype(F32) * out.astype(F32), axis=0, keepdims=True)
            for i, lane in zip(group, lanes):
                at = slice(starts[i] - starts[first], starts[i] - starts[first] + sizes[i])
                g_ref[:, lane] = low[:, at]
                d_ref[:, lane] = jnp.broadcast_to(delta[:, at], (8, sizes[i]))
            outer = outer + contract(out, rows, 1, 0)
        a_ref[...] = outer

    vmem = pl.BlockSpec(memory_space=pltpu.VMEM)
    return pl.pallas_call(
        body,
        in_specs=[pl.BlockSpec(memory_space=pltpu.SMEM)]
        + [pl.BlockSpec(memory_space=pltpu.VMEM)] * count
        + [pl.BlockSpec()] * (3 + len(earlier)),
        out_specs=[pl.BlockSpec()] * 3,
        out_shape=[
            jax.ShapeDtypeStruct((HEAD_DIM, total), BF16),
            jax.ShapeDtypeStruct((8, total), F32),
            jax.ShapeDtypeStruct((HEAD_DIM, width), F32),
        ],
        compiler_params=pltpu.CompilerParams(vmem_limit_bytes=24 * 2**20),
        cost_estimate=pl.CostEstimate(
            flops=4 * sum(sizes) * width * HEAD_DIM,
            bytes_accessed=2 * sum(sizes) * width,
            transcendentals=0,
        ),
        name="project",
    )(places, *pieces, gated, attended, inverse, *earlier)


def backward(which, low, grad, delta, query, key, value, parts, earlier):
    total = low.shape[0]
    half = total // parts // 2
    span = BLOCK // (2 * half)
    steps = total // BLOCK
    some = total // 2
    chunk = 1024

    def body(*refs):
        e_ref, g_ref, d_ref, q_ref, k_ref, v_ref = refs[:6]
        if which:
            dq_ref, extra_ref, o_ref, dk, dv = refs[6:]
        else:
            sum_ref, o_ref, dk, dv = refs[6:]
        step = pl.program_id(0)

        @pl.when(step == 0)
        def _():
            dk[...] = jnp.zeros_like(dk)
            dv[...] = jnp.zeros_like(dv)

        minus = -d_ref[0:1]
        high = minus.astype(BF16).astype(F32)
        row = lax.broadcasted_iota(jnp.int32, (HEAD_DIM, BLOCK), 0)
        extra = jnp.where(row == 0, high, jnp.where(row == 1, minus - high, 0.0)).astype(BF16)
        grad_block = g_ref[...]
        widened = jnp.concatenate([grad_block, extra], axis=0)
        grad_rows = grad_block.T
        query_rows = q_ref[...].T
        dq = dq_ref[...] if which else jnp.zeros((HEAD_DIM, BLOCK), F32)
        for first in range(0, some, chunk):
            rows = slice(first, first + chunk)
            dprob = contract(v_ref[rows, :], widened, 1, 0)
            probs = e_ref[rows, :]
            dscore = (probs.astype(F32) * dprob).astype(BF16)
            dq = dq + contract(k_ref[:, rows], dscore, 1, 0)
            dv[rows, :] += contract(probs, grad_rows, 1, 0)
            dk[rows, :] += contract(dscore, query_rows, 1, 0)
        if which:
            o_ref[pl.ds(step * span, span), : 2 * half, :] = (
                (dq * SCALE).T.astype(BF16).reshape(span, 2 * half, HEAD_DIM)
            )
        else:
            sum_ref[...] = dq

        @pl.when(step == steps - 1)
        def _():
            dk_low = (dk[...] * SCALE).astype(BF16).reshape(parts, half, HEAD_DIM)
            dv_low = dv[...].astype(BF16).reshape(parts, half, HEAD_DIM)
            if which:
                o_ref[:, 2 * half : 3 * half, :] = dk_low
                o_ref[:, 3 * half : 4 * half, :] = dv_low
                vector = extra_ref[...]
                first = vector.astype(BF16)
                rest = (vector - first.astype(F32)).astype(BF16)
                both = jnp.concatenate([first, rest], axis=0)
                o_ref[:, 4 * half :, :] = jnp.broadcast_to(both[None], (parts, 32, HEAD_DIM))
            else:
                o_ref[:, 0] = dk_low
                o_ref[:, 1] = dv_low

    column = lambda i: (0, i)
    shape = (parts, 4 * half + 32, HEAD_DIM) if which else (parts, 2, half, HEAD_DIM)
    out_specs = [pl.BlockSpec(shape, lambda i: (0,) * len(shape))]
    out_shape = [jax.ShapeDtypeStruct(shape, BF16)]
    more = []
    if which:
        more = [
            pl.BlockSpec((HEAD_DIM, BLOCK), column),
            pl.BlockSpec((16, HEAD_DIM), lambda i: (0, 0)),
        ]
    else:
        out_specs = [pl.BlockSpec((HEAD_DIM, BLOCK), column)] + out_specs
        out_shape = [jax.ShapeDtypeStruct((HEAD_DIM, total), F32)] + out_shape
    return pl.pallas_call(
        body,
        grid=(steps,),
        in_specs=[
            pl.BlockSpec((some, BLOCK), lambda i: (which, i)),
            pl.BlockSpec((HEAD_DIM, BLOCK), column),
            pl.BlockSpec((8, BLOCK), column),
            pl.BlockSpec((HEAD_DIM, BLOCK), column),
            pl.BlockSpec((HEAD_DIM, some), lambda i: (0, which)),
            pl.BlockSpec((some, 2 * HEAD_DIM), lambda i: (which, 0)),
        ]
        + more,
        out_specs=out_specs,
        out_shape=out_shape,
        scratch_shapes=[pltpu.VMEM((some, HEAD_DIM), F32)] * 2,
        compiler_params=PARAMS,
        cost_estimate=pl.CostEstimate(
            flops=5 * total * total * HEAD_DIM,
            bytes_accessed=total * total,
            transcendentals=0,
        ),
        name="backward",
    )(low, grad, delta, query, key, value, *earlier)


def swap(values, axis, size, bit):
    return lax.ppermute(values, axis, [(i, i ^ bit) for i in range(size)])


def total_over(values, axis):
    got = [values] + [swap(values, axis, 8, bit) for bit in range(1, 8)]
    while len(got) > 1:
        got = [got[i] + got[i + 1] for i in range(0, len(got), 2)]
    return got[0]


def after(token, arrays):
    anywhere = pl.BlockSpec(memory_space=pl.ANY)
    return pl.pallas_call(
        lambda *refs: None,
        in_specs=[anywhere] * (1 + len(arrays)),
        out_specs=[anywhere] * len(arrays),
        out_shape=[jax.ShapeDtypeStruct(x.shape, x.dtype) for x in arrays],
        input_output_aliases={i + 1: i for i in range(len(arrays))},
        name="after",
    )(token, *arrays)


def move(values, z_step=0, y_step=0, core_step=0):
    pairs = []
    for i in range(16):
        z, y, core = i // 4, i // 2 % 2, i % 2
        pairs.append((i, ((z + z_step) % 4 * 2 + (y ^ y_step)) * 2 + (core ^ core_step)))
    return lax.ppermute(values, "seq", pairs)


def shards(
    queries, key_rows, value_rows, cotangent, attn_gate, lengths, w_out, row_moment, col_moment
):
    seq_size = lax.axis_size("seq")
    dp_size = lax.axis_size("dp")
    inner_dim = queries.shape[2]
    width_dim = cotangent.shape[2]
    columns = width_dim // dp_size
    tokens = queries.shape[1]
    half = tokens // 2
    gate = attn_gate[0][None, :]

    own = cotangent[0]
    side = move(own, y_step=1)
    below, above = move(own, z_step=1), move(own, z_step=3)
    packed = split_columns([queries[0], key_rows[0], value_rows[0]])
    packed, side, below, above = lax.optimization_barrier((packed, side, below, above))
    packed = lax.all_to_all(packed, "seq", 0, 0, tiled=True)
    far_low, far_high = move(below[:half], z_step=1), move(above[half:], z_step=3)
    side_below, side_above = move(side, z_step=1), move(side, z_step=3)

    weight = w_out.astype(F32)
    gated = (weight * gate).astype(BF16)
    low, attended, query, inverse, key, value = forward(lengths, packed)
    side, below, above, far_low, far_high, side_below, side_above = after(
        inverse, [side, below, above, far_low, far_high, side_below, side_above]
    )
    side_low, side_high = move(side_below[:half], z_step=1), move(side_above[half:], z_step=3)
    found = [
        (own, 0, 0, 0),
        (side, 0, 1, 0),
        (below, 3, 0, 0),
        (above, 1, 0, 0),
        (far_low, 2, 0, 0),
        (far_high, 2, 0, half),
        (side_below, 3, 1, 0),
        (side_above, 1, 1, 0),
        (side_low, 2, 1, 0),
        (side_high, 2, 1, half),
    ]
    me = lax.axis_index("seq")
    z, y, core = me // 4, me // 2 % 2, me % 2
    made = []
    for some in (found[:4], found[4:]):
        pieces, places = [], []
        for core_step in range(2):
            for rows, z_step, y_step, offset in some:
                device = ((z + z_step) % 4 * 2 + (y ^ y_step)) * 2 + (core ^ core_step)
                pieces.append(move(rows, core_step=1) if core_step else rows)
                places.append(device * tokens + offset)
        made = project(
            jnp.stack(places).astype(jnp.int32), pieces, gated, attended, inverse, made
        )
    grad, delta, outer = made

    partial = (outer * gate).astype(BF16).reshape(HEAD_DIM, dp_size, columns)
    partial = lax.all_to_all(partial.transpose(1, 0, 2), "dp", 0, 0, tiled=True)
    some_q, early = backward(0, low, grad, delta, query, key, value, seq_size, [])
    some_q, early, partial = lax.optimization_barrier((some_q, early, partial))
    early = lax.all_to_all(early, "seq", 0, 0, tiled=True)
    grad_weight = jnp.sum(partial.astype(F32), axis=0)
    squares = grad_weight * grad_weight + EPSILON
    gate_part = jnp.sum(weight * outer, axis=0)
    row_total = total_over(jnp.sum(squares, axis=1), "dp")
    joined = jnp.concatenate(
        [gate_part, jnp.sum(squares, axis=0), jnp.zeros((320,), F32)]
    ).reshape(16, HEAD_DIM)
    (late,) = backward(
        1, low, grad, delta, query, key, value, seq_size, [some_q, joined]
    )
    early, late = lax.optimization_barrier((early, late))
    late = lax.all_to_all(late, "seq", 0, 0, tiled=True)
    grad_q, grad_k, grad_v, joined = join_columns(early, late)
    joined = joined.reshape(2048)
    row_new = 0.8 * row_moment + 0.2 * (row_total / width_dim)
    col_new = 0.8 * col_moment + 0.2 * (joined[width_dim : width_dim + columns] / inner_dim)
    return (
        grad_q[None],
        grad_k[None],
        grad_v[None],
        joined[:width_dim][None],
        grad_weight,
        row_new,
        col_new,
    )


def solution(mesh):
    tokens = P("dp", "seq", None)
    return jax.shard_map(
        shards,
        mesh=mesh,
        in_specs=(
            tokens,
            tokens,
            tokens,
            tokens,
            P("dp", None),
            P("dp"),
            P("seq", None),
            P("seq"),
            P("dp"),
        ),
        out_specs=(
            tokens,
            tokens,
            tokens,
            P("dp", None),
            P("seq", "dp"),
            P("seq"),
            P("dp"),
        ),
        check_vma=False,
    )
```

```python
import jax
import jax.numpy as jnp
from jax import lax
from jax.experimental import pallas as pl
from jax.experimental.pallas import tpu as pltpu
from jax.sharding import PartitionSpec as P

HEAD_DIM = 128
SCALE = 1.0 / HEAD_DIM**0.5
LOG2E = 1.4426950408889634
EPSILON = 1e-30
BLOCK = 512
BF16 = jnp.bfloat16
F32 = jnp.float32
PARAMS = pltpu.CompilerParams(vmem_limit_bytes=56 * 2**20)


def contract(left, right, left_dim, right_dim):
    return lax.dot_general(
        left, right, (((left_dim,), (right_dim,)), ((), ())), preferred_element_type=F32
    )


def split_columns(sources):
    tokens, inner = sources[0].shape
    heads = inner // HEAD_DIM
    count = len(sources)
    block = tokens // 4

    def body(*refs):
        out = refs[count]
        for which in range(count):
            for head in range(heads):
                out[head, which] = refs[which][:, head * HEAD_DIM : (head + 1) * HEAD_DIM]

    return pl.pallas_call(
        body,
        grid=(tokens // block,),
        in_specs=[pl.BlockSpec((block, inner), lambda i: (i, 0))] * count,
        out_specs=pl.BlockSpec((heads, count, block, HEAD_DIM), lambda i: (0, 0, i, 0)),
        out_shape=jax.ShapeDtypeStruct((heads, count, tokens, HEAD_DIM), BF16),
        name="split_columns",
    )(*sources)


def join_columns(early, late):
    heads, _, half, _ = early.shape
    inner = heads * HEAD_DIM

    def body(early_ref, late_ref, dq, dk, dv, sums):
        step = pl.program_id(0)
        for head in range(heads):
            lanes = slice(head * HEAD_DIM, (head + 1) * HEAD_DIM)
            dq[:, lanes] = late_ref[head, pl.ds(step * half, half), :]

        @pl.when(step == 0)
        def _():
            for head in range(heads):
                lanes = slice(head * HEAD_DIM, (head + 1) * HEAD_DIM)
                dk[:, lanes] = early_ref[head, 0]
                dv[:, lanes] = early_ref[head, 1]
            total = jnp.zeros((16, HEAD_DIM), F32)
            for head in range(heads):
                total = total + late_ref[head, 4 * half : 4 * half + 16, :].astype(F32)
                total = total + late_ref[head, 4 * half + 16 : 4 * half + 32, :].astype(F32)
            sums[...] = total

        @pl.when(step == 1)
        def _():
            for head in range(heads):
                lanes = slice(head * HEAD_DIM, (head + 1) * HEAD_DIM)
                dk[:, lanes] = late_ref[head, 2 * half : 3 * half, :]
                dv[:, lanes] = late_ref[head, 3 * half : 4 * half, :]

    rows = pl.BlockSpec((half, inner), lambda i: (i, 0))
    return pl.pallas_call(
        body,
        grid=(2,),
        in_specs=[pl.BlockSpec(memory_space=pltpu.VMEM)] * 2,
        out_specs=[rows, rows, rows, pl.BlockSpec((16, HEAD_DIM), lambda i: (0, 0))],
        out_shape=[jax.ShapeDtypeStruct((2 * half, inner), BF16)] * 3
        + [jax.ShapeDtypeStruct((16, HEAD_DIM), F32)],
        compiler_params=pltpu.CompilerParams(vmem_limit_bytes=16 * 2**20),
        name="join_columns",
    )(early, late)


def forward(valid_len, packed):
    parts, _, tokens, _ = packed.shape
    total = parts * tokens
    span = BLOCK // tokens
    steps = total // BLOCK
    chunk = 512

    def body(
        len_ref, p_ref, e_ref, att_ref, qt_ref, inv_ref, kt_ref, va_ref, ka, vt, held, tops
    ):
        step = pl.program_id(0)
        length = len_ref[0]

        @pl.when(step == 0)
        def _():
            half = tokens // 2
            some = total // 2
            row = lax.broadcasted_iota(jnp.int32, (some, HEAD_DIM), 0)
            col = lax.broadcasted_iota(jnp.int32, (some, HEAD_DIM), 1)
            vt[HEAD_DIM:, :] = jnp.ones((16, total), BF16)
            for part in range(2):
                of = slice(part * half, (part + 1) * half)
                at = slice(part * some, (part + 1) * some)
                key_rows = p_ref[:, 1, of, :].reshape(some, HEAD_DIM)
                value_rows = p_ref[:, 2, of, :].reshape(some, HEAD_DIM)
                slot = row // half * tokens + part * half + row % half
                ka[at, :HEAD_DIM] = key_rows
                ka[at, HEAD_DIM:] = jnp.where((slot >= length) & (col == 0), -1e30, 0.0).astype(
                    BF16
                )
                vt[:HEAD_DIM, at] = value_rows.T
                kt_ref[:, at] = key_rows.T
                va_ref[at, :HEAD_DIM] = value_rows
                va_ref[at, HEAD_DIM:] = jnp.where(col < 2, 1.0, 0.0).astype(BF16)

        def live(block):
            slot = block * BLOCK + lax.broadcasted_iota(jnp.int32, (1, BLOCK), 1)
            return slot < length

        def work(score_next, weigh_last):
            if score_next:
                query = p_ref[pl.ds(step * span, span), 0]
                query = query.reshape(BLOCK, HEAD_DIM).T
                qt_ref[...] = query
                row = lax.broadcasted_iota(jnp.int32, (HEAD_DIM, BLOCK), 0)
                extra = jnp.where(row == 0, 1.0, 0.0).astype(BF16)
                widened = jnp.concatenate([query, extra], axis=0)
                top = jnp.full((8, BLOCK), -3e38, F32)
            if weigh_last:
                shift = tops[0:1]
                summed = jnp.zeros((HEAD_DIM + 16, BLOCK), F32)
            for first in range(0, total, chunk):
                rows = slice(first, first + chunk)
                if weigh_last:
                    low = jnp.exp2(held[rows, :] * (SCALE * LOG2E) - shift).astype(BF16)
                    e_ref[rows, :] = low
                if score_next:
                    scores = contract(ka[rows, :], widened, 1, 0)
                    held[rows, :] = scores
                    top = jnp.maximum(top, jnp.max(scores.reshape(chunk // 8, 8, BLOCK), axis=0))
                if weigh_last:
                    summed = summed + contract(vt[:, rows], low, 1, 0)
            if weigh_last:
                inverse = jnp.where(live(step - 1), 1.0 / summed[HEAD_DIM : HEAD_DIM + 1], 0.0)
                att_ref[...] = (summed[:HEAD_DIM] * inverse).astype(BF16)
                inv_ref[...] = jnp.broadcast_to(inverse, (8, BLOCK))
            if score_next:
                top = jnp.max(top, axis=0, keepdims=True) * (SCALE * LOG2E)
                tops[...] = jnp.broadcast_to(jnp.where(live(step), top, 1e30), (8, BLOCK))

        pl.when(step == 0)(lambda: work(True, False))
        pl.when((step > 0) & (step < steps))(lambda: work(True, True))
        pl.when(step == steps)(lambda: work(False, True))

    whole = lambda i, n: (0, 0)
    scored = lambda i, n: (0, jnp.minimum(i, steps - 1))
    weighed = lambda i, n: (0, jnp.maximum(i - 1, 0))
    return pl.pallas_call(
        body,
        grid_spec=pltpu.PrefetchScalarGridSpec(
            num_scalar_prefetch=1,
            grid=(steps + 1,),
            in_specs=[
                pl.BlockSpec(memory_space=pltpu.VMEM),
            ],
            out_specs=[
                pl.BlockSpec((total, BLOCK), weighed),
                pl.BlockSpec((HEAD_DIM, BLOCK), weighed),
                pl.BlockSpec((HEAD_DIM, BLOCK), scored),
                pl.BlockSpec((8, BLOCK), weighed),
                pl.BlockSpec((HEAD_DIM, total), whole),
                pl.BlockSpec((total, 2 * HEAD_DIM), whole),
            ],
            scratch_shapes=[
                pltpu.VMEM((total, 2 * HEAD_DIM), BF16),
                pltpu.VMEM((HEAD_DIM + 16, total), BF16),
                pltpu.VMEM((total, BLOCK), F32),
                pltpu.VMEM((8, BLOCK), F32),
            ],
        ),
        out_shape=[
            pltpu.HBM((total, total), BF16),
            pltpu.HBM((HEAD_DIM, total), BF16),
            pltpu.HBM((HEAD_DIM, total), BF16),
            pltpu.HBM((8, total), F32),
            pltpu.HBM((HEAD_DIM, total), BF16),
            pltpu.HBM((total, 2 * HEAD_DIM), BF16),
        ],
        compiler_params=pltpu.CompilerParams(vmem_limit_bytes=40 * 2**20),
        cost_estimate=pl.CostEstimate(
            flops=6 * total * total * HEAD_DIM,
            bytes_accessed=2 * total * total,
            transcendentals=total * total,
        ),
        name="forward",
    )(valid_len, packed)


def project(places, pieces, gated, attended, inverse, earlier):
    width = gated.shape[1]
    total = attended.shape[1]
    count = len(pieces)
    sizes = [piece.shape[0] for piece in pieces]
    starts = [sum(sizes[:i]) for i in range(count)]
    groups, filled = [[]], 0
    for i in range(count):
        if filled == 1024:
            groups.append([])
            filled = 0
        groups[-1].append(i)
        filled += sizes[i]

    def body(*refs):
        place_ref, sources = refs[0], refs[1 : 1 + count]
        w_ref, o_ref, inv_ref = refs[1 + count : 4 + count]
        before = refs[4 + count : 4 + count + len(earlier)]
        g_ref, d_ref, a_ref = refs[4 + count + len(earlier) :]
        outer = jnp.zeros((HEAD_DIM, width), F32)
        if before:
            g_ref[...] = before[0][...]
            d_ref[...] = before[1][...]
            outer = before[2][...]
        for group in groups:
            lanes = [
                pl.ds(pl.multiple_of(place_ref[i], HEAD_DIM), sizes[i]) for i in group
            ]
            out = jnp.concatenate([o_ref[:, lane] for lane in lanes], axis=1)
            inv = jnp.concatenate([inv_ref[0:1, lane] for lane in lanes], axis=1)
            first = group[0]
            rows = jnp.concatenate([sources[i][...] for i in group], axis=0)
            grad = contract(w_ref[...], rows, 1, 1).astype(BF16).astype(F32)
            low = (grad * inv).astype(BF16)
            delta = jnp.sum(low.astype(F32) * out.astype(F32), axis=0, keepdims=True)
            for i, lane in zip(group, lanes):
                at = slice(starts[i] - starts[first], starts[i] - starts[first] + sizes[i])
                g_ref[:, lane] = low[:, at]
                d_ref[:, lane] = jnp.broadcast_to(delta[:, at], (8, sizes[i]))
            outer = outer + contract(out, rows, 1, 0)
        a_ref[...] = outer

    vmem = pl.BlockSpec(memory_space=pltpu.VMEM)
    return pl.pallas_call(
        body,
        in_specs=[pl.BlockSpec(memory_space=pltpu.SMEM)]
        + [pl.BlockSpec(memory_space=pltpu.VMEM)] * count
        + [pl.BlockSpec()] * (3 + len(earlier)),
        out_specs=[pl.BlockSpec()] * 3,
        out_shape=[
            pltpu.HBM((HEAD_DIM, total), BF16),
            pltpu.HBM((8, total), F32),
            pltpu.HBM((HEAD_DIM, width), F32),
        ],
        compiler_params=pltpu.CompilerParams(vmem_limit_bytes=24 * 2**20),
        cost_estimate=pl.CostEstimate(
            flops=4 * sum(sizes) * width * HEAD_DIM,
            bytes_accessed=2 * sum(sizes) * width,
            transcendentals=0,
        ),
        name="project",
    )(places, *pieces, gated, attended, inverse, *earlier)


def backward(which, low, grad, delta, query, key, value, parts, earlier):
    total = low.shape[0]
    half = total // parts // 2
    span = BLOCK // (2 * half)
    steps = total // BLOCK
    some = total // 2
    chunk = 1024

    def body(*refs):
        e_ref, g_ref, d_ref, q_ref, k_ref, v_ref = refs[:6]
        if which:
            dq_ref, extra_ref, o_ref, dk, dv = refs[6:]
        else:
            sum_ref, o_ref, dk, dv = refs[6:]
        step = pl.program_id(0)

        @pl.when(step == 0)
        def _():
            dk[...] = jnp.zeros_like(dk)
            dv[...] = jnp.zeros_like(dv)

        minus = -d_ref[0:1]
        high = minus.astype(BF16).astype(F32)
        row = lax.broadcasted_iota(jnp.int32, (HEAD_DIM, BLOCK), 0)
        extra = jnp.where(row == 0, high, jnp.where(row == 1, minus - high, 0.0)).astype(BF16)
        grad_block = g_ref[...]
        widened = jnp.concatenate([grad_block, extra], axis=0)
        grad_rows = grad_block.T
        query_rows = q_ref[...].T
        dq = dq_ref[...] if which else jnp.zeros((HEAD_DIM, BLOCK), F32)
        for first in range(0, some, chunk):
            rows = slice(first, first + chunk)
            dprob = contract(v_ref[rows, :], widened, 1, 0)
            probs = e_ref[rows, :]
            dscore = (probs.astype(F32) * dprob).astype(BF16)
            dq = dq + contract(k_ref[:, rows], dscore, 1, 0)
            dv[rows, :] += contract(probs, grad_rows, 1, 0)
            dk[rows, :] += contract(dscore, query_rows, 1, 0)
        if which:
            o_ref[pl.ds(step * span, span), : 2 * half, :] = (
                (dq * SCALE).T.astype(BF16).reshape(span, 2 * half, HEAD_DIM)
            )
        else:
            sum_ref[...] = dq

        @pl.when(step == steps - 1)
        def _():
            dk_low = (dk[...] * SCALE).astype(BF16).reshape(parts, half, HEAD_DIM)
            dv_low = dv[...].astype(BF16).reshape(parts, half, HEAD_DIM)
            if which:
                o_ref[:, 2 * half : 3 * half, :] = dk_low
                o_ref[:, 3 * half : 4 * half, :] = dv_low
                vector = extra_ref[...]
                first = vector.astype(BF16)
                rest = (vector - first.astype(F32)).astype(BF16)
                both = jnp.concatenate([first, rest], axis=0)
                o_ref[:, 4 * half :, :] = jnp.broadcast_to(both[None], (parts, 32, HEAD_DIM))
            else:
                o_ref[:, 0] = dk_low
                o_ref[:, 1] = dv_low

    column = lambda i: (0, i)
    shape = (parts, 4 * half + 32, HEAD_DIM) if which else (parts, 2, half, HEAD_DIM)
    out_specs = [pl.BlockSpec(shape, lambda i: (0,) * len(shape))]
    out_shape = [jax.ShapeDtypeStruct(shape, BF16)]
    more = []
    if which:
        more = [
            pl.BlockSpec((HEAD_DIM, BLOCK), column),
            pl.BlockSpec((16, HEAD_DIM), lambda i: (0, 0)),
        ]
    else:
        out_specs = [pl.BlockSpec((HEAD_DIM, BLOCK), column)] + out_specs
        out_shape = [jax.ShapeDtypeStruct((HEAD_DIM, total), F32)] + out_shape
    return pl.pallas_call(
        body,
        grid=(steps,),
        in_specs=[
            pl.BlockSpec((some, BLOCK), lambda i: (which, i)),
            pl.BlockSpec((HEAD_DIM, BLOCK), column),
            pl.BlockSpec((8, BLOCK), column),
            pl.BlockSpec((HEAD_DIM, BLOCK), column),
            pl.BlockSpec((HEAD_DIM, some), lambda i: (0, which)),
            pl.BlockSpec((some, 2 * HEAD_DIM), lambda i: (which, 0)),
        ]
        + more,
        out_specs=out_specs,
        out_shape=out_shape,
        scratch_shapes=[pltpu.VMEM((some, HEAD_DIM), F32)] * 2,
        compiler_params=PARAMS,
        cost_estimate=pl.CostEstimate(
            flops=5 * total * total * HEAD_DIM,
            bytes_accessed=total * total,
            transcendentals=0,
        ),
        name="backward",
    )(low, grad, delta, query, key, value, *earlier)


def swap(values, axis, size, bit):
    return lax.ppermute(values, axis, [(i, i ^ bit) for i in range(size)])


def total_over(values, axis):
    one, two, three = (swap(values, axis, 8, bit) for bit in (1, 2, 3))
    values = (values + one) + (two + three)
    return values + swap(values, axis, 8, 4)


def after(token, arrays):
    anywhere = pl.BlockSpec(memory_space=pl.ANY)
    return pl.pallas_call(
        lambda *refs: None,
        in_specs=[anywhere] * (1 + len(arrays)),
        out_specs=[anywhere] * len(arrays),
        out_shape=[jax.ShapeDtypeStruct(x.shape, x.dtype) for x in arrays],
        input_output_aliases={i + 1: i for i in range(len(arrays))},
        name="after",
    )(token, *arrays)


def move(values, z_step=0, y_step=0, core_step=0):
    pairs = []
    for i in range(16):
        z, y, core = i // 4, i // 2 % 2, i % 2
        pairs.append((i, ((z + z_step) % 4 * 2 + (y ^ y_step)) * 2 + (core ^ core_step)))
    return lax.ppermute(values, "seq", pairs)


def shards(
    queries, key_rows, value_rows, cotangent, attn_gate, lengths, w_out, row_moment, col_moment
):
    seq_size = lax.axis_size("seq")
    dp_size = lax.axis_size("dp")
    inner_dim = queries.shape[2]
    width_dim = cotangent.shape[2]
    columns = width_dim // dp_size
    tokens = queries.shape[1]
    half = tokens // 2
    gate = attn_gate[0][None, :]

    own = cotangent[0]
    side = move(own, y_step=1)
    below, above = move(own, z_step=1), move(own, z_step=3)
    packed = split_columns([queries[0], key_rows[0], value_rows[0]])
    packed, side, below, above = lax.optimization_barrier((packed, side, below, above))
    packed = lax.all_to_all(packed, "seq", 0, 0, tiled=True)
    far_low, far_high = move(below[:half], z_step=1), move(above[half:], z_step=3)
    side_below, side_above = move(side, z_step=1), move(side, z_step=3)

    weight = w_out.astype(F32)
    gated = (weight * gate).astype(BF16)
    low, attended, query, inverse, key, value = forward(lengths, packed)
    side, below, above, far_low, far_high, side_below, side_above = after(
        inverse, [side, below, above, far_low, far_high, side_below, side_above]
    )
    side_low, side_high = move(side_below[:half], z_step=1), move(side_above[half:], z_step=3)
    found = [
        (own, 0, 0, 0),
        (side, 0, 1, 0),
        (below, 3, 0, 0),
        (above, 1, 0, 0),
        (far_low, 2, 0, 0),
        (far_high, 2, 0, half),
        (side_below, 3, 1, 0),
        (side_above, 1, 1, 0),
        (side_low, 2, 1, 0),
        (side_high, 2, 1, half),
    ]
    me = lax.axis_index("seq")
    z, y, core = me // 4, me // 2 % 2, me % 2
    made = []
    for some in (found[:4], found[4:]):
        if made:
            late = after(made[1], [side_low, side_high])
            some = some[:4] + [(late[0],) + some[4][1:], (late[1],) + some[5][1:]]
        pieces, places = [], []
        for core_step in range(2):
            for rows, z_step, y_step, offset in some:
                device = ((z + z_step) % 4 * 2 + (y ^ y_step)) * 2 + (core ^ core_step)
                pieces.append(move(rows, core_step=1) if core_step else rows)
                places.append(device * tokens + offset)
        made = project(
            jnp.stack(places).astype(jnp.int32), pieces, gated, attended, inverse, made
        )
    grad, delta, outer = made

    partial = (outer * gate).astype(BF16).reshape(HEAD_DIM, dp_size, columns)
    partial = lax.all_to_all(partial.transpose(1, 0, 2), "dp", 0, 0, tiled=True)
    some_q, early = backward(0, low, grad, delta, query, key, value, seq_size, [])
    some_q, early, partial = lax.optimization_barrier((some_q, early, partial))
    early = lax.all_to_all(early, "seq", 0, 0, tiled=True)
    grad_weight = jnp.sum(partial.astype(F32), axis=0)
    squares = grad_weight * grad_weight + EPSILON
    gate_part = jnp.sum(weight * outer, axis=0)
    row_total = total_over(jnp.sum(squares, axis=1), "dp")
    joined = jnp.concatenate(
        [gate_part, jnp.sum(squares, axis=0), jnp.zeros((320,), F32)]
    ).reshape(16, HEAD_DIM)
    (late,) = backward(
        1, low, grad, delta, query, key, value, seq_size, [some_q, joined]
    )
    early, late = lax.optimization_barrier((early, late))
    late = lax.all_to_all(late, "seq", 0, 0, tiled=True)
    grad_q, grad_k, grad_v, joined = join_columns(early, late)
    joined = joined.reshape(2048)
    row_new = 0.8 * row_moment + 0.2 * (row_total / width_dim)
    col_new = 0.8 * col_moment + 0.2 * (joined[width_dim : width_dim + columns] / inner_dim)
    return (
        grad_q[None],
        grad_k[None],
        grad_v[None],
        joined[:width_dim][None],
        grad_weight,
        row_new,
        col_new,
    )


def solution(mesh):
    tokens = P("dp", "seq", None)
    return jax.shard_map(
        shards,
        mesh=mesh,
        in_specs=(
            tokens,
            tokens,
            tokens,
            tokens,
            P("dp", None),
            P("dp"),
            P("seq", None),
            P("seq"),
            P("dp"),
        ),
        out_specs=(
            tokens,
            tokens,
            tokens,
            P("dp", None),
            P("seq", "dp"),
            P("seq"),
            P("dp"),
        ),
        check_vma=False,
    )
```

```python
import jax
import jax.numpy as jnp
from jax import lax
from jax.experimental import pallas as pl
from jax.experimental.pallas import tpu as pltpu
from jax.sharding import PartitionSpec as P

HEAD_DIM = 128
SCALE = 1.0 / HEAD_DIM**0.5
LOG2E = 1.4426950408889634
EPSILON = 1e-30
BLOCK = 512
BF16 = jnp.bfloat16
F32 = jnp.float32
PARAMS = pltpu.CompilerParams(vmem_limit_bytes=56 * 2**20)


def contract(left, right, left_dim, right_dim):
    return lax.dot_general(
        left, right, (((left_dim,), (right_dim,)), ((), ())), preferred_element_type=F32
    )


def split_columns(sources):
    tokens, inner = sources[0].shape
    heads = inner // HEAD_DIM
    count = len(sources)
    block = tokens // 4

    def body(*refs):
        out = refs[count]
        for which in range(count):
            for head in range(heads):
                out[head, which] = refs[which][:, head * HEAD_DIM : (head + 1) * HEAD_DIM]

    return pl.pallas_call(
        body,
        grid=(tokens // block,),
        in_specs=[pl.BlockSpec((block, inner), lambda i: (i, 0))] * count,
        out_specs=pl.BlockSpec((heads, count, block, HEAD_DIM), lambda i: (0, 0, i, 0)),
        out_shape=jax.ShapeDtypeStruct((heads, count, tokens, HEAD_DIM), BF16),
        name="split_columns",
    )(*sources)


def join_columns(early, late):
    heads, _, half, _ = early.shape
    inner = heads * HEAD_DIM

    def body(early_ref, late_ref, dq, dk, dv, sums):
        step = pl.program_id(0)
        for head in range(heads):
            lanes = slice(head * HEAD_DIM, (head + 1) * HEAD_DIM)
            dq[:, lanes] = late_ref[head, pl.ds(step * half, half), :]

        @pl.when(step == 0)
        def _():
            for head in range(heads):
                lanes = slice(head * HEAD_DIM, (head + 1) * HEAD_DIM)
                dk[:, lanes] = early_ref[head, 0]
                dv[:, lanes] = early_ref[head, 1]
            total = jnp.zeros((16, HEAD_DIM), F32)
            for head in range(heads):
                total = total + late_ref[head, 4 * half : 4 * half + 16, :].astype(F32)
                total = total + late_ref[head, 4 * half + 16 : 4 * half + 32, :].astype(F32)
            sums[...] = total

        @pl.when(step == 1)
        def _():
            for head in range(heads):
                lanes = slice(head * HEAD_DIM, (head + 1) * HEAD_DIM)
                dk[:, lanes] = late_ref[head, 2 * half : 3 * half, :]
                dv[:, lanes] = late_ref[head, 3 * half : 4 * half, :]

    rows = pl.BlockSpec((half, inner), lambda i: (i, 0))
    return pl.pallas_call(
        body,
        grid=(2,),
        in_specs=[pl.BlockSpec(memory_space=pltpu.VMEM)] * 2,
        out_specs=[rows, rows, rows, pl.BlockSpec((16, HEAD_DIM), lambda i: (0, 0))],
        out_shape=[jax.ShapeDtypeStruct((2 * half, inner), BF16)] * 3
        + [jax.ShapeDtypeStruct((16, HEAD_DIM), F32)],
        compiler_params=pltpu.CompilerParams(vmem_limit_bytes=16 * 2**20),
        name="join_columns",
    )(early, late)


def forward(valid_len, packed):
    parts, _, tokens, _ = packed.shape
    total = parts * tokens
    span = BLOCK // tokens
    steps = total // BLOCK
    chunk = 512

    def body(
        len_ref, p_ref, e_ref, att_ref, qt_ref, inv_ref, kt_ref, va_ref, ka, vt, held, tops
    ):
        step = pl.program_id(0)
        length = len_ref[0]

        @pl.when(step == 0)
        def _():
            half = tokens // 2
            some = total // 2
            row = lax.broadcasted_iota(jnp.int32, (some, HEAD_DIM), 0)
            col = lax.broadcasted_iota(jnp.int32, (some, HEAD_DIM), 1)
            vt[HEAD_DIM:, :] = jnp.ones((16, total), BF16)
            for part in range(2):
                of = slice(part * half, (part + 1) * half)
                at = slice(part * some, (part + 1) * some)
                key_rows = p_ref[:, 1, of, :].reshape(some, HEAD_DIM)
                value_rows = p_ref[:, 2, of, :].reshape(some, HEAD_DIM)
                slot = row // half * tokens + part * half + row % half
                ka[at, :HEAD_DIM] = key_rows
                ka[at, HEAD_DIM:] = jnp.where((slot >= length) & (col == 0), -1e30, 0.0).astype(
                    BF16
                )
                vt[:HEAD_DIM, at] = value_rows.T
                kt_ref[:, at] = key_rows.T
                va_ref[at, :HEAD_DIM] = value_rows
                va_ref[at, HEAD_DIM:] = jnp.where(col < 2, 1.0, 0.0).astype(BF16)

        def live(block):
            slot = block * BLOCK + lax.broadcasted_iota(jnp.int32, (1, BLOCK), 1)
            return slot < length

        def work(score_next, weigh_last):
            if score_next:
                query = p_ref[pl.ds(step * span, span), 0]
                query = query.reshape(BLOCK, HEAD_DIM).T
                qt_ref[...] = query
                row = lax.broadcasted_iota(jnp.int32, (HEAD_DIM, BLOCK), 0)
                extra = jnp.where(row == 0, 1.0, 0.0).astype(BF16)
                widened = jnp.concatenate([query, extra], axis=0)
                top = jnp.full((8, BLOCK), -3e38, F32)
            if weigh_last:
                shift = tops[0:1]
                summed = jnp.zeros((HEAD_DIM + 16, BLOCK), F32)
            for first in range(0, total, chunk):
                rows = slice(first, first + chunk)
                if weigh_last:
                    low = jnp.exp2(held[rows, :] * (SCALE * LOG2E) - shift).astype(BF16)
                    e_ref[rows, :] = low
                if score_next:
                    scores = contract(ka[rows, :], widened, 1, 0)
                    held[rows, :] = scores
                    top = jnp.maximum(top, jnp.max(scores.reshape(chunk // 8, 8, BLOCK), axis=0))
                if weigh_last:
                    summed = summed + contract(vt[:, rows], low, 1, 0)
            if weigh_last:
                inverse = jnp.where(live(step - 1), 1.0 / summed[HEAD_DIM : HEAD_DIM + 1], 0.0)
                att_ref[...] = (summed[:HEAD_DIM] * inverse).astype(BF16)
                inv_ref[...] = jnp.broadcast_to(inverse, (8, BLOCK))
            if score_next:
                top = jnp.max(top, axis=0, keepdims=True) * (SCALE * LOG2E)
                tops[...] = jnp.broadcast_to(jnp.where(live(step), top, 1e30), (8, BLOCK))

        pl.when(step == 0)(lambda: work(True, False))
        pl.when((step > 0) & (step < steps))(lambda: work(True, True))
        pl.when(step == steps)(lambda: work(False, True))

    whole = lambda i, n: (0, 0)
    scored = lambda i, n: (0, jnp.minimum(i, steps - 1))
    weighed = lambda i, n: (0, jnp.maximum(i - 1, 0))
    return pl.pallas_call(
        body,
        grid_spec=pltpu.PrefetchScalarGridSpec(
            num_scalar_prefetch=1,
            grid=(steps + 1,),
            in_specs=[
                pl.BlockSpec(memory_space=pltpu.VMEM),
            ],
            out_specs=[
                pl.BlockSpec((total, BLOCK), weighed),
                pl.BlockSpec((HEAD_DIM, BLOCK), weighed),
                pl.BlockSpec((HEAD_DIM, BLOCK), scored),
                pl.BlockSpec((8, BLOCK), weighed),
                pl.BlockSpec((HEAD_DIM, total), whole),
                pl.BlockSpec((total, 2 * HEAD_DIM), whole),
            ],
            scratch_shapes=[
                pltpu.VMEM((total, 2 * HEAD_DIM), BF16),
                pltpu.VMEM((HEAD_DIM + 16, total), BF16),
                pltpu.VMEM((total, BLOCK), F32),
                pltpu.VMEM((8, BLOCK), F32),
            ],
        ),
        out_shape=[
            pltpu.HBM((total, total), BF16),
            pltpu.HBM((HEAD_DIM, total), BF16),
            pltpu.HBM((HEAD_DIM, total), BF16),
            pltpu.HBM((8, total), F32),
            pltpu.HBM((HEAD_DIM, total), BF16),
            pltpu.HBM((total, 2 * HEAD_DIM), BF16),
        ],
        compiler_params=pltpu.CompilerParams(vmem_limit_bytes=40 * 2**20),
        cost_estimate=pl.CostEstimate(
            flops=6 * total * total * HEAD_DIM,
            bytes_accessed=2 * total * total,
            transcendentals=total * total,
        ),
        name="forward",
    )(valid_len, packed)


def project(places, pieces, gated, attended, inverse, earlier, gate=None):
    width = gated.shape[1]
    total = attended.shape[1]
    count = len(pieces)
    eighth = width // 8
    operands = list(earlier) + ([] if gate is None else [gate])
    sizes = [piece.shape[0] for piece in pieces]
    starts = [sum(sizes[:i]) for i in range(count)]
    groups, filled = [[]], 0
    for i in range(count):
        if filled == 1024:
            groups.append([])
            filled = 0
        groups[-1].append(i)
        filled += sizes[i]

    def body(*refs):
        place_ref, sources = refs[0], refs[1 : 1 + count]
        w_ref, o_ref, inv_ref = refs[1 + count : 4 + count]
        before = refs[4 + count : 4 + count + len(earlier)]
        outs = refs[4 + count + len(operands) :]
        g_ref, d_ref, a_ref = outs[:3]
        held, sems = outs[-2:]
        copies = [
            pltpu.make_async_copy(
                sources[i], held.at[pl.ds(starts[i], sizes[i]), :], sems.at[i]
            )
            for i in range(count)
        ]
        for copy in copies:
            copy.start()
        outer = jnp.zeros((HEAD_DIM, width), F32)
        if before:
            g_ref[...] = before[0][...]
            d_ref[...] = before[1][...]
            outer = before[2][...]
        for group in groups:
            lanes = [
                pl.ds(pl.multiple_of(place_ref[i], HEAD_DIM), sizes[i]) for i in group
            ]
            out = jnp.concatenate([o_ref[:, lane] for lane in lanes], axis=1)
            inv = jnp.concatenate([inv_ref[0:1, lane] for lane in lanes], axis=1)
            first = group[0]
            last = group[-1]
            for i in group:
                copies[i].wait()
            rows = held[starts[first] : starts[last] + sizes[last], :]
            grad = contract(w_ref[...], rows, 1, 1).astype(BF16).astype(F32)
            low = (grad * inv).astype(BF16)
            delta = jnp.sum(low.astype(F32) * out.astype(F32), axis=0, keepdims=True)
            for i, lane in zip(group, lanes):
                at = slice(starts[i] - starts[first], starts[i] - starts[first] + sizes[i])
                g_ref[:, lane] = low[:, at]
                d_ref[:, lane] = jnp.broadcast_to(delta[:, at], (8, sizes[i]))
            outer = outer + contract(out, rows, 1, 0)
        a_ref[...] = outer
        if gate is not None:
            partial = (outer * refs[4 + count + len(earlier)][...]).astype(BF16)
            for i in range(8):
                outs[3][i] = partial[:, i * eighth : (i + 1) * eighth]

    out_shape = [
        pltpu.HBM((HEAD_DIM, total), BF16),
        pltpu.HBM((8, total), F32),
        pltpu.HBM((HEAD_DIM, width), F32),
    ]
    if gate is not None:
        out_shape.append(pltpu.HBM((8, HEAD_DIM, eighth), BF16))
    return pl.pallas_call(
        body,
        in_specs=[pl.BlockSpec(memory_space=pltpu.SMEM)]
        + [pl.BlockSpec(memory_space=pl.ANY)] * count
        + [pl.BlockSpec()] * (3 + len(operands)),
        out_specs=[pl.BlockSpec()] * len(out_shape),
        out_shape=out_shape,
        scratch_shapes=[
            pltpu.VMEM((sum(sizes), width), BF16),
            pltpu.SemaphoreType.DMA((count,)),
        ],
        compiler_params=pltpu.CompilerParams(vmem_limit_bytes=24 * 2**20),
        cost_estimate=pl.CostEstimate(
            flops=4 * sum(sizes) * width * HEAD_DIM,
            bytes_accessed=2 * sum(sizes) * width,
            transcendentals=0,
        ),
        name="project",
    )(
        places,
        *[pltpu.with_memory_space_constraint(x, pltpu.HBM) for x in pieces],
        gated,
        *[
            pltpu.with_memory_space_constraint(x, pltpu.HBM)
            for x in [attended, inverse] + operands
        ],
    )


def backward(which, low, grad, delta, query, key, value, parts, earlier):
    total = low.shape[0]
    half = total // parts // 2
    span = BLOCK // (2 * half)
    steps = total // BLOCK
    some = total // 2
    chunk = 1024

    def body(*refs):
        e_ref, g_ref, d_ref, q_ref, k_ref, v_ref = refs[:6]
        if which:
            dq_ref, extra_ref, o_ref, dk, dv = refs[6:]
        else:
            sum_ref, o_ref, dk, dv = refs[6:]
        step = pl.program_id(0)

        @pl.when(step == 0)
        def _():
            dk[...] = jnp.zeros_like(dk)
            dv[...] = jnp.zeros_like(dv)

        minus = -d_ref[0:1]
        high = minus.astype(BF16).astype(F32)
        row = lax.broadcasted_iota(jnp.int32, (HEAD_DIM, BLOCK), 0)
        extra = jnp.where(row == 0, high, jnp.where(row == 1, minus - high, 0.0)).astype(BF16)
        grad_block = g_ref[...]
        widened = jnp.concatenate([grad_block, extra], axis=0)
        grad_rows = grad_block.T
        query_rows = q_ref[...].T
        dq = dq_ref[...] if which else jnp.zeros((HEAD_DIM, BLOCK), F32)
        for first in range(0, some, chunk):
            rows = slice(first, first + chunk)
            dprob = contract(v_ref[rows, :], widened, 1, 0)
            probs = e_ref[rows, :]
            dscore = (probs.astype(F32) * dprob).astype(BF16)
            dq = dq + contract(k_ref[:, rows], dscore, 1, 0)
            dv[rows, :] += contract(probs, grad_rows, 1, 0)
            dk[rows, :] += contract(dscore, query_rows, 1, 0)
        if which:
            o_ref[pl.ds(step * span, span), : 2 * half, :] = (
                (dq * SCALE).T.astype(BF16).reshape(span, 2 * half, HEAD_DIM)
            )
        else:
            sum_ref[...] = dq

        @pl.when(step == steps - 1)
        def _():
            dk_low = (dk[...] * SCALE).astype(BF16).reshape(parts, half, HEAD_DIM)
            dv_low = dv[...].astype(BF16).reshape(parts, half, HEAD_DIM)
            if which:
                o_ref[:, 2 * half : 3 * half, :] = dk_low
                o_ref[:, 3 * half : 4 * half, :] = dv_low
                vector = extra_ref[...]
                first = vector.astype(BF16)
                rest = (vector - first.astype(F32)).astype(BF16)
                both = jnp.concatenate([first, rest], axis=0)
                o_ref[:, 4 * half :, :] = jnp.broadcast_to(both[None], (parts, 32, HEAD_DIM))
            else:
                o_ref[:, 0] = dk_low
                o_ref[:, 1] = dv_low

    column = lambda i: (0, i)
    shape = (parts, 4 * half + 32, HEAD_DIM) if which else (parts, 2, half, HEAD_DIM)
    out_specs = [pl.BlockSpec(shape, lambda i: (0,) * len(shape))]
    out_shape = [jax.ShapeDtypeStruct(shape, BF16)]
    more = []
    if which:
        more = [
            pl.BlockSpec((HEAD_DIM, BLOCK), column),
            pl.BlockSpec((16, HEAD_DIM), lambda i: (0, 0)),
        ]
    else:
        out_specs = [pl.BlockSpec((HEAD_DIM, BLOCK), column)] + out_specs
        out_shape = [jax.ShapeDtypeStruct((HEAD_DIM, total), F32)] + out_shape
    return pl.pallas_call(
        body,
        grid=(steps,),
        in_specs=[
            pl.BlockSpec((some, BLOCK), lambda i: (which, i)),
            pl.BlockSpec((HEAD_DIM, BLOCK), column),
            pl.BlockSpec((8, BLOCK), column),
            pl.BlockSpec((HEAD_DIM, BLOCK), column),
            pl.BlockSpec((HEAD_DIM, some), lambda i: (0, which)),
            pl.BlockSpec((some, 2 * HEAD_DIM), lambda i: (which, 0)),
        ]
        + more,
        out_specs=out_specs,
        out_shape=out_shape,
        scratch_shapes=[pltpu.VMEM((some, HEAD_DIM), F32)] * 2,
        compiler_params=PARAMS,
        cost_estimate=pl.CostEstimate(
            flops=5 * total * total * HEAD_DIM,
            bytes_accessed=total * total,
            transcendentals=0,
        ),
        name="backward",
    )(low, grad, delta, query, key, value, *earlier)


def swap(values, axis, size, bit):
    return lax.ppermute(values, axis, [(i, i ^ bit) for i in range(size)])


def total_over(values, axis):
    one, two, three = (swap(values, axis, 8, bit) for bit in (1, 2, 3))
    values = (values + one) + (two + three)
    return values + swap(values, axis, 8, 4)


def after(token, arrays):
    anywhere = pl.BlockSpec(memory_space=pl.ANY)
    return pl.pallas_call(
        lambda *refs: None,
        in_specs=[anywhere] * (1 + len(arrays)),
        out_specs=[anywhere] * len(arrays),
        out_shape=[pltpu.HBM(x.shape, x.dtype) for x in arrays],
        input_output_aliases={i + 1: i for i in range(len(arrays))},
        name="after",
    )(token, *[pltpu.with_memory_space_constraint(x, pltpu.HBM) for x in arrays])


def move(values, z_step=0, y_step=0, core_step=0):
    pairs = []
    for i in range(16):
        z, y, core = i // 4, i // 2 % 2, i % 2
        pairs.append((i, ((z + z_step) % 4 * 2 + (y ^ y_step)) * 2 + (core ^ core_step)))
    return lax.ppermute(values, "seq", pairs)


def shards(
    queries, key_rows, value_rows, cotangent, attn_gate, lengths, w_out, row_moment, col_moment
):
    seq_size = lax.axis_size("seq")
    dp_size = lax.axis_size("dp")
    inner_dim = queries.shape[2]
    width_dim = cotangent.shape[2]
    columns = width_dim // dp_size
    tokens = queries.shape[1]
    half = tokens // 2
    gate = attn_gate[0][None, :]

    own = cotangent[0]
    side = move(own, y_step=1)
    below, above = move(own, z_step=1), move(own, z_step=3)
    packed = split_columns([queries[0], key_rows[0], value_rows[0]])
    packed, side, below, above = lax.optimization_barrier((packed, side, below, above))
    packed = lax.all_to_all(packed, "seq", 0, 0, tiled=True)
    far_low, far_high = move(below[:half], z_step=1), move(above[half:], z_step=3)
    side_below, side_above = move(side, z_step=1), move(side, z_step=3)

    weight = w_out.astype(F32)
    gated = (weight * gate).astype(BF16)
    low, attended, query, inverse, key, value = forward(lengths, packed)
    side, below, above, far_low, far_high, side_below, side_above = after(
        inverse, [side, below, above, far_low, far_high, side_below, side_above]
    )
    side_low, side_high = move(far_low, y_step=1), move(far_high, y_step=1)
    found = [
        (own, 0, 0, 0),
        (side, 0, 1, 0),
        (below, 3, 0, 0),
        (above, 1, 0, 0),
        (far_low, 2, 0, 0),
        (far_high, 2, 0, half),
        (side_below, 3, 1, 0),
        (side_above, 1, 1, 0),
        (side_low, 2, 1, 0),
        (side_high, 2, 1, half),
    ]
    me = lax.axis_index("seq")
    z, y, core = me // 4, me // 2 % 2, me % 2
    made = []
    for some in (found[:4], found[4:]):
        if made:
            late = after(made[1], [side_low, side_high])
            some = some[:4] + [(late[0],) + some[4][1:], (late[1],) + some[5][1:]]
        pieces, places = [], []
        for core_step in range(2):
            for rows, z_step, y_step, offset in some:
                device = ((z + z_step) % 4 * 2 + (y ^ y_step)) * 2 + (core ^ core_step)
                pieces.append(move(rows, core_step=1) if core_step else rows)
                places.append(device * tokens + offset)
        made = project(
            jnp.stack(places).astype(jnp.int32),
            pieces,
            gated,
            attended,
            inverse,
            made,
            gate if made else None,
        )
    grad, delta, outer, partial = made
    partial = lax.all_to_all(partial, "dp", 0, 0, tiled=True)
    some_q, early = backward(0, low, grad, delta, query, key, value, seq_size, [])
    some_q, early, partial = lax.optimization_barrier((some_q, early, partial))
    early = lax.all_to_all(early, "seq", 0, 0, tiled=True)
    grad_weight = jnp.sum(partial.astype(F32), axis=0)
    squares = grad_weight * grad_weight + EPSILON
    gate_part = jnp.sum(weight * outer, axis=0)
    row_total = total_over(jnp.sum(squares, axis=1), "dp")
    joined = jnp.concatenate(
        [gate_part, jnp.sum(squares, axis=0), jnp.zeros((320,), F32)]
    ).reshape(16, HEAD_DIM)
    (late,) = backward(
        1, low, grad, delta, query, key, value, seq_size, [some_q, joined]
    )
    early, late = lax.optimization_barrier((early, late))
    late = lax.all_to_all(late, "seq", 0, 0, tiled=True)
    grad_q, grad_k, grad_v, joined = join_columns(early, late)
    joined = joined.reshape(2048)
    row_new = 0.8 * row_moment + 0.2 * (row_total / width_dim)
    col_new = 0.8 * col_moment + 0.2 * (joined[width_dim : width_dim + columns] / inner_dim)
    return (
        grad_q[None],
        grad_k[None],
        grad_v[None],
        joined[:width_dim][None],
        grad_weight,
        row_new,
        col_new,
    )


def solution(mesh):
    tokens = P("dp", "seq", None)
    return jax.shard_map(
        shards,
        mesh=mesh,
        in_specs=(
            tokens,
            tokens,
            tokens,
            tokens,
            P("dp", None),
            P("dp"),
            P("seq", None),
            P("seq"),
            P("dp"),
        ),
        out_specs=(
            tokens,
            tokens,
            tokens,
            P("dp", None),
            P("seq", "dp"),
            P("seq"),
            P("dp"),
        ),
        check_vma=False,
    )
```

```python
import jax
import jax.numpy as jnp
from jax import lax
from jax.experimental import pallas as pl
from jax.experimental.pallas import tpu as pltpu
from jax.sharding import PartitionSpec as P

HEAD_DIM = 128
SCALE = 1.0 / HEAD_DIM**0.5
LOG2E = 1.4426950408889634
EPSILON = 1e-30
BLOCK = 512
BF16 = jnp.bfloat16
F32 = jnp.float32
PARAMS = pltpu.CompilerParams(vmem_limit_bytes=56 * 2**20)


def contract(left, right, left_dim, right_dim):
    return lax.dot_general(
        left, right, (((left_dim,), (right_dim,)), ((), ())), preferred_element_type=F32
    )


def split_columns(sources):
    tokens, inner = sources[0].shape
    heads = inner // HEAD_DIM
    count = len(sources)
    block = tokens // 4

    def body(*refs):
        out = refs[count]
        for which in range(count):
            for head in range(heads):
                out[head, which] = refs[which][:, head * HEAD_DIM : (head + 1) * HEAD_DIM]

    return pl.pallas_call(
        body,
        grid=(tokens // block,),
        in_specs=[pl.BlockSpec((block, inner), lambda i: (i, 0))] * count,
        out_specs=pl.BlockSpec((heads, count, block, HEAD_DIM), lambda i: (0, 0, i, 0)),
        out_shape=jax.ShapeDtypeStruct((heads, count, tokens, HEAD_DIM), BF16),
        name="split_columns",
    )(*sources)


def join_columns(early, late):
    heads, _, half, _ = early.shape
    inner = heads * HEAD_DIM

    def body(early_ref, late_ref, dq, dk, dv, sums):
        step = pl.program_id(0)
        for head in range(heads):
            lanes = slice(head * HEAD_DIM, (head + 1) * HEAD_DIM)
            dq[:, lanes] = late_ref[head, pl.ds(step * half, half), :]

        @pl.when(step == 0)
        def _():
            for head in range(heads):
                lanes = slice(head * HEAD_DIM, (head + 1) * HEAD_DIM)
                dk[:, lanes] = early_ref[head, 0]
                dv[:, lanes] = early_ref[head, 1]
            total = jnp.zeros((16, HEAD_DIM), F32)
            for head in range(heads):
                total = total + late_ref[head, 4 * half : 4 * half + 16, :].astype(F32)
                total = total + late_ref[head, 4 * half + 16 : 4 * half + 32, :].astype(F32)
            sums[...] = total

        @pl.when(step == 1)
        def _():
            for head in range(heads):
                lanes = slice(head * HEAD_DIM, (head + 1) * HEAD_DIM)
                dk[:, lanes] = late_ref[head, 2 * half : 3 * half, :]
                dv[:, lanes] = late_ref[head, 3 * half : 4 * half, :]

    rows = pl.BlockSpec((half, inner), lambda i: (i, 0))
    return pl.pallas_call(
        body,
        grid=(2,),
        in_specs=[pl.BlockSpec(memory_space=pltpu.VMEM)] * 2,
        out_specs=[rows, rows, rows, pl.BlockSpec((16, HEAD_DIM), lambda i: (0, 0))],
        out_shape=[jax.ShapeDtypeStruct((2 * half, inner), BF16)] * 3
        + [jax.ShapeDtypeStruct((16, HEAD_DIM), F32)],
        compiler_params=pltpu.CompilerParams(vmem_limit_bytes=16 * 2**20),
        name="join_columns",
    )(early, late)


def forward(valid_len, packed):
    parts, _, tokens, _ = packed.shape
    total = parts * tokens
    span = BLOCK // tokens
    steps = total // BLOCK
    chunk = 512

    def body(
        len_ref, p_ref, e_ref, att_ref, qt_ref, inv_ref, kt_ref, va_ref, ka, vt, held, tops
    ):
        step = pl.program_id(0)
        length = len_ref[0]

        @pl.when(step == 0)
        def _():
            half = tokens // 2
            some = total // 2
            row = lax.broadcasted_iota(jnp.int32, (some, HEAD_DIM), 0)
            col = lax.broadcasted_iota(jnp.int32, (some, HEAD_DIM), 1)
            vt[HEAD_DIM:, :] = jnp.ones((16, total), BF16)
            for part in range(2):
                of = slice(part * half, (part + 1) * half)
                at = slice(part * some, (part + 1) * some)
                key_rows = p_ref[:, 1, of, :].reshape(some, HEAD_DIM)
                value_rows = p_ref[:, 2, of, :].reshape(some, HEAD_DIM)
                slot = row // half * tokens + part * half + row % half
                ka[at, :HEAD_DIM] = key_rows
                ka[at, HEAD_DIM:] = jnp.where((slot >= length) & (col == 0), -1e30, 0.0).astype(
                    BF16
                )
                vt[:HEAD_DIM, at] = value_rows.T
                kt_ref[:, at] = key_rows.T
                va_ref[at, :HEAD_DIM] = value_rows
                va_ref[at, HEAD_DIM:] = jnp.where(col < 2, 1.0, 0.0).astype(BF16)

        def live(block):
            slot = block * BLOCK + lax.broadcasted_iota(jnp.int32, (1, BLOCK), 1)
            return slot < length

        def work(score_next, weigh_last):
            if score_next:
                query = p_ref[pl.ds(step * span, span), 0]
                query = query.reshape(BLOCK, HEAD_DIM).T
                qt_ref[...] = query
                row = lax.broadcasted_iota(jnp.int32, (HEAD_DIM, BLOCK), 0)
                extra = jnp.where(row == 0, 1.0, 0.0).astype(BF16)
                widened = jnp.concatenate([query, extra], axis=0)
                top = jnp.full((8, BLOCK), -3e38, F32)
            if weigh_last:
                shift = tops[0:1]
                summed = jnp.zeros((HEAD_DIM + 16, BLOCK), F32)
            for first in range(0, total, chunk):
                rows = slice(first, first + chunk)
                if weigh_last:
                    low = jnp.exp2(held[rows, :] * (SCALE * LOG2E) - shift).astype(BF16)
                    e_ref[rows, :] = low
                if score_next:
                    scores = contract(ka[rows, :], widened, 1, 0)
                    held[rows, :] = scores
                    top = jnp.maximum(top, jnp.max(scores.reshape(chunk // 8, 8, BLOCK), axis=0))
                if weigh_last:
                    summed = summed + contract(vt[:, rows], low, 1, 0)
            if weigh_last:
                inverse = jnp.where(live(step - 1), 1.0 / summed[HEAD_DIM : HEAD_DIM + 1], 0.0)
                att_ref[...] = (summed[:HEAD_DIM] * inverse).astype(BF16)
                inv_ref[...] = jnp.broadcast_to(inverse, (8, BLOCK))
            if score_next:
                top = jnp.max(top, axis=0, keepdims=True) * (SCALE * LOG2E)
                tops[...] = jnp.broadcast_to(jnp.where(live(step), top, 1e30), (8, BLOCK))

        pl.when(step == 0)(lambda: work(True, False))
        pl.when((step > 0) & (step < steps))(lambda: work(True, True))
        pl.when(step == steps)(lambda: work(False, True))

    whole = lambda i, n: (0, 0)
    scored = lambda i, n: (0, jnp.minimum(i, steps - 1))
    weighed = lambda i, n: (0, jnp.maximum(i - 1, 0))
    return pl.pallas_call(
        body,
        grid_spec=pltpu.PrefetchScalarGridSpec(
            num_scalar_prefetch=1,
            grid=(steps + 1,),
            in_specs=[
                pl.BlockSpec(memory_space=pltpu.VMEM),
            ],
            out_specs=[
                pl.BlockSpec((total, BLOCK), weighed),
                pl.BlockSpec((HEAD_DIM, BLOCK), weighed),
                pl.BlockSpec((HEAD_DIM, BLOCK), scored),
                pl.BlockSpec((8, BLOCK), weighed),
                pl.BlockSpec((HEAD_DIM, total), whole),
                pl.BlockSpec((total, 2 * HEAD_DIM), whole),
            ],
            scratch_shapes=[
                pltpu.VMEM((total, 2 * HEAD_DIM), BF16),
                pltpu.VMEM((HEAD_DIM + 16, total), BF16),
                pltpu.VMEM((total, BLOCK), F32),
                pltpu.VMEM((8, BLOCK), F32),
            ],
        ),
        out_shape=[
            pltpu.HBM((total, total), BF16),
            pltpu.HBM((HEAD_DIM, total), BF16),
            pltpu.HBM((HEAD_DIM, total), BF16),
            pltpu.HBM((8, total), F32),
            pltpu.HBM((HEAD_DIM, total), BF16),
            pltpu.HBM((total, 2 * HEAD_DIM), BF16),
        ],
        compiler_params=pltpu.CompilerParams(vmem_limit_bytes=40 * 2**20),
        cost_estimate=pl.CostEstimate(
            flops=6 * total * total * HEAD_DIM,
            bytes_accessed=2 * total * total,
            transcendentals=total * total,
        ),
        name="forward",
    )(valid_len, packed)


def project(places, pieces, gated, attended, inverse, earlier, gate=None):
    width = gated.shape[1]
    total = attended.shape[1]
    count = len(pieces)
    eighth = width // 8
    operands = list(earlier) + ([] if gate is None else [gate])
    sizes = [piece.shape[0] for piece in pieces]
    starts = [sum(sizes[:i]) for i in range(count)]
    groups, filled = [[]], 0
    for i in range(count):
        if filled == 1024:
            groups.append([])
            filled = 0
        groups[-1].append(i)
        filled += sizes[i]

    def body(*refs):
        place_ref, sources = refs[0], refs[1 : 1 + count]
        w_ref, o_ref, inv_ref = refs[1 + count : 4 + count]
        before = refs[4 + count : 4 + count + len(earlier)]
        outs = refs[4 + count + len(operands) :]
        g_ref, d_ref, a_ref = outs[:3]
        held, sems = outs[-2:]
        copies = [
            pltpu.make_async_copy(
                sources[i], held.at[pl.ds(starts[i], sizes[i]), :], sems.at[i]
            )
            for i in range(count)
        ]
        for copy in copies:
            copy.start()
        outer = jnp.zeros((HEAD_DIM, width), F32)
        if before:
            g_ref[...] = before[0][...]
            d_ref[...] = before[1][...]
            outer = before[2][...]
        for group in groups:
            lanes = [
                pl.ds(pl.multiple_of(place_ref[i], HEAD_DIM), sizes[i]) for i in group
            ]
            out = jnp.concatenate([o_ref[:, lane] for lane in lanes], axis=1)
            inv = jnp.concatenate([inv_ref[0:1, lane] for lane in lanes], axis=1)
            first = group[0]
            last = group[-1]
            for i in group:
                copies[i].wait()
            rows = held[starts[first] : starts[last] + sizes[last], :]
            grad = contract(w_ref[...], rows, 1, 1).astype(BF16).astype(F32)
            low = (grad * inv).astype(BF16)
            delta = jnp.sum(low.astype(F32) * out.astype(F32), axis=0, keepdims=True)
            for i, lane in zip(group, lanes):
                at = slice(starts[i] - starts[first], starts[i] - starts[first] + sizes[i])
                g_ref[:, lane] = low[:, at]
                d_ref[:, lane] = jnp.broadcast_to(delta[:, at], (8, sizes[i]))
            outer = outer + contract(out, rows, 1, 0)
        a_ref[...] = outer
        if gate is not None:
            partial = (outer * refs[4 + count + len(earlier)][...]).T.astype(BF16)
            outs[3][...] = partial.reshape(8, eighth, HEAD_DIM)

    out_shape = [
        pltpu.HBM((HEAD_DIM, total), BF16),
        pltpu.HBM((8, total), F32),
        pltpu.HBM((HEAD_DIM, width), F32),
    ]
    if gate is not None:
        out_shape.append(pltpu.HBM((8, eighth, HEAD_DIM), BF16))
    return pl.pallas_call(
        body,
        in_specs=[pl.BlockSpec(memory_space=pltpu.SMEM)]
        + [pl.BlockSpec(memory_space=pl.ANY)] * count
        + [pl.BlockSpec()] * (3 + len(operands)),
        out_specs=[pl.BlockSpec()] * len(out_shape),
        out_shape=out_shape,
        scratch_shapes=[
            pltpu.VMEM((sum(sizes), width), BF16),
            pltpu.SemaphoreType.DMA((count,)),
        ],
        compiler_params=pltpu.CompilerParams(vmem_limit_bytes=24 * 2**20),
        cost_estimate=pl.CostEstimate(
            flops=4 * sum(sizes) * width * HEAD_DIM,
            bytes_accessed=2 * sum(sizes) * width,
            transcendentals=0,
        ),
        name="project",
    )(
        places,
        *[pltpu.with_memory_space_constraint(x, pltpu.HBM) for x in pieces],
        gated,
        *[
            pltpu.with_memory_space_constraint(x, pltpu.HBM)
            for x in [attended, inverse] + operands
        ],
    )


def backward(which, low, grad, delta, query, key, value, parts, earlier):
    total = low.shape[0]
    half = total // parts // 2
    span = BLOCK // (2 * half)
    steps = total // BLOCK
    some = total // 2
    chunk = 1024

    def body(*refs):
        e_ref, g_ref, d_ref, q_ref, k_ref, v_ref = refs[:6]
        if which:
            dq_ref, extra_ref, o_ref, dk, dv = refs[6:]
        else:
            sum_ref, o_ref, dk, dv = refs[6:]
        step = pl.program_id(0)

        @pl.when(step == 0)
        def _():
            dk[...] = jnp.zeros_like(dk)
            dv[...] = jnp.zeros_like(dv)

        minus = -d_ref[0:1]
        high = minus.astype(BF16).astype(F32)
        row = lax.broadcasted_iota(jnp.int32, (HEAD_DIM, BLOCK), 0)
        extra = jnp.where(row == 0, high, jnp.where(row == 1, minus - high, 0.0)).astype(BF16)
        grad_block = g_ref[...]
        widened = jnp.concatenate([grad_block, extra], axis=0)
        grad_rows = grad_block.T
        query_rows = q_ref[...].T
        dq = dq_ref[...] if which else jnp.zeros((HEAD_DIM, BLOCK), F32)
        for first in range(0, some, chunk):
            rows = slice(first, first + chunk)
            dprob = contract(v_ref[rows, :], widened, 1, 0)
            probs = e_ref[rows, :]
            dscore = (probs.astype(F32) * dprob).astype(BF16)
            dq = dq + contract(k_ref[:, rows], dscore, 1, 0)
            dv[rows, :] += contract(probs, grad_rows, 1, 0)
            dk[rows, :] += contract(dscore, query_rows, 1, 0)
        if which:
            o_ref[pl.ds(step * span, span), : 2 * half, :] = (
                (dq * SCALE).T.astype(BF16).reshape(span, 2 * half, HEAD_DIM)
            )
        else:
            sum_ref[...] = dq

        @pl.when(step == steps - 1)
        def _():
            dk_low = (dk[...] * SCALE).astype(BF16).reshape(parts, half, HEAD_DIM)
            dv_low = dv[...].astype(BF16).reshape(parts, half, HEAD_DIM)
            if which:
                o_ref[:, 2 * half : 3 * half, :] = dk_low
                o_ref[:, 3 * half : 4 * half, :] = dv_low
                vector = extra_ref[...]
                first = vector.astype(BF16)
                rest = (vector - first.astype(F32)).astype(BF16)
                both = jnp.concatenate([first, rest], axis=0)
                o_ref[:, 4 * half :, :] = jnp.broadcast_to(both[None], (parts, 32, HEAD_DIM))
            else:
                o_ref[:, 0] = dk_low
                o_ref[:, 1] = dv_low

    column = lambda i: (0, i)
    shape = (parts, 4 * half + 32, HEAD_DIM) if which else (parts, 2, half, HEAD_DIM)
    out_specs = [pl.BlockSpec(shape, lambda i: (0,) * len(shape))]
    out_shape = [jax.ShapeDtypeStruct(shape, BF16)]
    more = []
    if which:
        more = [
            pl.BlockSpec((HEAD_DIM, BLOCK), column),
            pl.BlockSpec((16, HEAD_DIM), lambda i: (0, 0)),
        ]
    else:
        out_specs = [pl.BlockSpec((HEAD_DIM, BLOCK), column)] + out_specs
        out_shape = [jax.ShapeDtypeStruct((HEAD_DIM, total), F32)] + out_shape
    return pl.pallas_call(
        body,
        grid=(steps,),
        in_specs=[
            pl.BlockSpec((some, BLOCK), lambda i: (which, i)),
            pl.BlockSpec((HEAD_DIM, BLOCK), column),
            pl.BlockSpec((8, BLOCK), column),
            pl.BlockSpec((HEAD_DIM, BLOCK), column),
            pl.BlockSpec((HEAD_DIM, some), lambda i: (0, which)),
            pl.BlockSpec((some, 2 * HEAD_DIM), lambda i: (which, 0)),
        ]
        + more,
        out_specs=out_specs,
        out_shape=out_shape,
        scratch_shapes=[pltpu.VMEM((some, HEAD_DIM), F32)] * 2,
        compiler_params=PARAMS,
        cost_estimate=pl.CostEstimate(
            flops=5 * total * total * HEAD_DIM,
            bytes_accessed=total * total,
            transcendentals=0,
        ),
        name="backward",
    )(low, grad, delta, query, key, value, *earlier)


def swap(values, axis, size, bit):
    return lax.ppermute(values, axis, [(i, i ^ bit) for i in range(size)])


def total_over(values, axis):
    one, two, three = (swap(values, axis, 8, bit) for bit in (1, 2, 3))
    values = (values + one) + (two + three)
    return values + swap(values, axis, 8, 4)


def after(token, arrays):
    anywhere = pl.BlockSpec(memory_space=pl.ANY)
    return pl.pallas_call(
        lambda *refs: None,
        in_specs=[anywhere] * (1 + len(arrays)),
        out_specs=[anywhere] * len(arrays),
        out_shape=[pltpu.HBM(x.shape, x.dtype) for x in arrays],
        input_output_aliases={i + 1: i for i in range(len(arrays))},
        name="after",
    )(token, *[pltpu.with_memory_space_constraint(x, pltpu.HBM) for x in arrays])


def move(values, z_step=0, y_step=0, core_step=0):
    pairs = []
    for i in range(16):
        z, y, core = i // 4, i // 2 % 2, i % 2
        pairs.append((i, ((z + z_step) % 4 * 2 + (y ^ y_step)) * 2 + (core ^ core_step)))
    return lax.ppermute(values, "seq", pairs)


def shards(
    queries, key_rows, value_rows, cotangent, attn_gate, lengths, w_out, row_moment, col_moment
):
    seq_size = lax.axis_size("seq")
    dp_size = lax.axis_size("dp")
    inner_dim = queries.shape[2]
    width_dim = cotangent.shape[2]
    columns = width_dim // dp_size
    tokens = queries.shape[1]
    half = tokens // 2
    gate = attn_gate[0][None, :]

    own = cotangent[0]
    side = move(own, y_step=1)
    below, above = move(own, z_step=1), move(own, z_step=3)
    packed = split_columns([queries[0], key_rows[0], value_rows[0]])
    packed, side, below, above = lax.optimization_barrier((packed, side, below, above))
    packed = lax.all_to_all(packed, "seq", 0, 0, tiled=True)
    far_low, far_high = move(below[:half], z_step=1), move(above[half:], z_step=3)
    side_below, side_above = move(side, z_step=1), move(side, z_step=3)

    weight = w_out.astype(F32)
    gated = (weight * gate).astype(BF16)
    low, attended, query, inverse, key, value = forward(lengths, packed)
    side, below, above, far_low, far_high, side_below, side_above = after(
        inverse, [side, below, above, far_low, far_high, side_below, side_above]
    )
    side_low, side_high = move(side_below[:half], z_step=1), move(side_above[half:], z_step=3)
    found = [
        (own, 0, 0, 0),
        (side, 0, 1, 0),
        (below, 3, 0, 0),
        (above, 1, 0, 0),
        (far_low, 2, 0, 0),
        (far_high, 2, 0, half),
        (side_below, 3, 1, 0),
        (side_above, 1, 1, 0),
        (side_low, 2, 1, 0),
        (side_high, 2, 1, half),
    ]
    me = lax.axis_index("seq")
    z, y, core = me // 4, me // 2 % 2, me % 2
    made = []
    for some in (found[:4], found[4:]):
        if made:
            late = after(made[1], [side_low, side_high])
            some = some[:4] + [(late[0],) + some[4][1:], (late[1],) + some[5][1:]]
        pieces, places = [], []
        for core_step in range(2):
            for rows, z_step, y_step, offset in some:
                device = ((z + z_step) % 4 * 2 + (y ^ y_step)) * 2 + (core ^ core_step)
                pieces.append(move(rows, core_step=1) if core_step else rows)
                places.append(device * tokens + offset)
        made = project(
            jnp.stack(places).astype(jnp.int32),
            pieces,
            gated,
            attended,
            inverse,
            made,
            gate if made else None,
        )
    grad, delta, outer, partial = made
    partial = lax.all_to_all(partial, "dp", 0, 0, tiled=True)
    some_q, early = backward(0, low, grad, delta, query, key, value, seq_size, [])
    some_q, early, partial = lax.optimization_barrier((some_q, early, partial))
    early = lax.all_to_all(early, "seq", 0, 0, tiled=True)
    grad_weight = jnp.sum(partial.astype(F32), axis=0).T
    squares = grad_weight * grad_weight + EPSILON
    gate_part = jnp.sum(weight * outer, axis=0)
    row_total = total_over(jnp.sum(squares, axis=1), "dp")
    joined = jnp.concatenate(
        [gate_part, jnp.sum(squares, axis=0), jnp.zeros((320,), F32)]
    ).reshape(16, HEAD_DIM)
    (late,) = backward(
        1, low, grad, delta, query, key, value, seq_size, [some_q, joined]
    )
    early, late = lax.optimization_barrier((early, late))
    late = lax.all_to_all(late, "seq", 0, 0, tiled=True)
    grad_q, grad_k, grad_v, joined = join_columns(early, late)
    joined = joined.reshape(2048)
    row_new = 0.8 * row_moment + 0.2 * (row_total / width_dim)
    col_new = 0.8 * col_moment + 0.2 * (joined[width_dim : width_dim + columns] / inner_dim)
    return (
        grad_q[None],
        grad_k[None],
        grad_v[None],
        joined[:width_dim][None],
        grad_weight,
        row_new,
        col_new,
    )


def solution(mesh):
    tokens = P("dp", "seq", None)
    return jax.shard_map(
        shards,
        mesh=mesh,
        in_specs=(
            tokens,
            tokens,
            tokens,
            tokens,
            P("dp", None),
            P("dp"),
            P("seq", None),
            P("seq"),
            P("dp"),
        ),
        out_specs=(
            tokens,
            tokens,
            tokens,
            P("dp", None),
            P("seq", "dp"),
            P("seq"),
            P("dp"),
        ),
        check_vma=False,
    )
```
